256 devices in a mesh: gx: 64 (over z, y, x_lo), gy: 4 (over x_hi, core).
Axes of the slice: x: 4 (x_hi: 2, x_lo: 2; x = x_hi * 2 + x_lo), y: 4, z: 8, core: 2. Of those that a mesh axis runs over, the one named last changes fastest.
Arguments:
- inputs: bfloat16 [4, 1536, 64, 512], P(None, 'gx', 'gy'), may hold values from -6 to 6
- coverage: int32 [1536, 64], P(None, 'gy'), may hold values from 0 to 1, as said below
- encoded: bfloat16 [64, 8, 64, 512], P('gx', 'gy'), may hold values from -6 to 6
- cross_list: int32 [192, 8, 4], P('gx', 'gy'), may hold values from 0 to 511, as said below
- gain_self: float32 [512], replicated, may hold values from 0.1 to 1.9
- gain_cross: float32 [512], replicated, may hold values from 0.1 to 1.9
- gain_ffn: float32 [512], replicated, may hold values from 0.1 to 1.9
- self_wq: bfloat16 [512, 512], replicated, may hold values from -1.5 to 1.5
- self_wkv: bfloat16 [512, 1024], replicated, may hold values from -1.5 to 1.5
- self_wo: bfloat16 [512, 512], replicated, may hold values from -0.25 to 0.25
- cross_wq: bfloat16 [512, 512], replicated, may hold values from -1.5 to 1.5
- cross_wkv: bfloat16 [512, 1024], replicated, may hold values from -1.5 to 1.5
- cross_wo: bfloat16 [512, 512], replicated, may hold values from -0.25 to 0.25
- ffn_in: bfloat16 [512, 2048], replicated, may hold values from -0.25 to 0.25
- ffn_out: bfloat16 [2048, 512], replicated, may hold values from -0.125 to 0.125
Outputs:
- output: bfloat16 [4, 1536, 64, 512], P(None, 'gx', 'gy')
The draws below stay inside these ranges and needn't reach their ends.
Inputs may be any that keep to these rules, and one draw needn't show every extreme that they name: 1 marks a cell with radar coverage. `cross_list`: for query cuboid (i, j), every entry e satisfies |e // 8 - i * 8 // 24| <= 1.
All inputs are finite; a program needn't handle non-finite values.
Results may differ from the reference program's by a relative error of at most 0.023.
Values may be sent and summed in bfloat16 or wider, within the bound.
No kernel may reach another device: no remote copies, remote signals or barrier semaphores. Data moves between devices by JAX's collectives and lax.ppermute only.
A program may use at most 128 MiB of HBM per device.

```python
import jax
import jax.numpy as jnp
from jax import lax

D = 512
HEADS = 8
FFN = 2048
FRAMES = 4
BX = 8
BY = 8
CX = 24
ETOK = 64
LIST = 4
NX = 1536
NY = 64
QX = 192
QY = 8
ECY = 8
N_GX = 64


weight_bound = 1.5


def draw_self_wq(key, part):
    key = jax.random.fold_in(key, 11)
    weight = jax.random.normal(key, (D, D), jnp.float32) * D ** (-0.5)
    return jnp.clip(weight, -weight_bound, weight_bound).astype(jnp.bfloat16)


def draw_self_wkv(key, part):
    key = jax.random.fold_in(key, 12)
    weight = jax.random.normal(key, (D, 2 * D), jnp.float32) * D ** (-0.5)
    return jnp.clip(weight, -weight_bound, weight_bound).astype(jnp.bfloat16)


def draw_cross_wq(key, part):
    key = jax.random.fold_in(key, 13)
    weight = jax.random.normal(key, (D, D), jnp.float32) * D ** (-0.5)
    return jnp.clip(weight, -weight_bound, weight_bound).astype(jnp.bfloat16)


def draw_cross_wkv(key, part):
    key = jax.random.fold_in(key, 14)
    weight = jax.random.normal(key, (D, 2 * D), jnp.float32) * D ** (-0.5)
    return jnp.clip(weight, -weight_bound, weight_bound).astype(jnp.bfloat16)


def draw_coverage(key, part):
    key = jax.random.fold_in(key, 21)
    key_one, key_two = jax.random.split(key)
    strips = NX // CX
    levels = jax.random.randint(key_one, (strips, 1), 10, 101)
    cell_draws = jax.random.randint(key_two, (strips, CX * NY), 0, 100)
    return (cell_draws < levels).astype(jnp.int32).reshape(NX, NY)


def draw_cross_list(key, part):
    key = jax.random.fold_in(key, 22)
    key_one, key_two = jax.random.split(key)
    strips = NX // CX
    home_strip = jnp.arange(QX, dtype=jnp.int32) * BX // CX
    offsets = jax.random.randint(key_one, (QX, QY, LIST), -1, 2)
    column = jnp.clip(home_strip[:, None, None] + offsets, 0, strips - 1)
    row_pick = jax.random.randint(key_two, (QX, QY, LIST), 0, ECY)
    entries = (column * ECY + row_pick).astype(jnp.int32)
    entries = entries.at[0, 0, 0].set(0)
    entries = entries.at[QX - 1, QY - 1, 0].set(strips * ECY - 1)
    return entries


def block_scale(stream_key, extent, shards, low, top_value):
    def one(position, blocks):
        heights = jax.random.uniform(jax.random.fold_in(jax.random.fold_in(stream_key, 6), position), (blocks,), jnp.float32, low / len(shards), top_value / len(shards))
        return jnp.repeat(jnp.exp(heights), extent[position] // blocks).reshape((-1,) + (1,) * (len(extent) - position - 1))

    level = one(*shards[0])
    for cut in shards[1:]:
        level = level * one(*cut)
    return level


def bell_draw(rng, extent, deviation, most, pieces=(), held_as=jnp.bfloat16):
    loudness = block_scale(rng, extent, pieces, -0.22, 0.18) if pieces else 1.0
    values = jax.random.normal(rng, extent, jnp.float32) * deviation * loudness
    return jnp.minimum(jnp.maximum(values, -most), most).astype(held_as)


def setup_inputs(seed: int = 0) -> dict:
    key_list = jax.random.split(jax.random.key(seed), 16)
    inputs = bell_draw(key_list[0], (FRAMES, NX, NY, D), 1.0, 6.0, ((1, 64), (2, 4)))
    coverage = draw_coverage(jax.random.fold_in(key_list[15], 71), 0)
    encoded = bell_draw(key_list[2], (N_GX, ECY, ETOK, D), 1.0, 6.0, ((0, 64), (1, 4)))
    cross_list = draw_cross_list(jax.random.fold_in(key_list[15], 71), 0)
    gain_self = jnp.clip(1.0 + 0.18 * jax.random.normal(key_list[4], (D,), jnp.float32), 0.1, 1.9)
    gain_cross = jnp.clip(1.0 + 0.18 * jax.random.normal(key_list[5], (D,), jnp.float32), 0.1, 1.9)
    gain_ffn = jnp.clip(1.0 + 0.18 * jax.random.normal(key_list[6], (D,), jnp.float32), 0.1, 1.9)
    self_wq = draw_self_wq(jax.random.fold_in(key_list[15], 71), 0)
    self_wkv = draw_self_wkv(jax.random.fold_in(key_list[15], 71), 0)
    self_wo = bell_draw(key_list[9], (D, D), D ** -0.5, 0.25)
    cross_wq = draw_cross_wq(jax.random.fold_in(key_list[15], 71), 0)
    cross_wkv = draw_cross_wkv(jax.random.fold_in(key_list[15], 71), 0)
    cross_wo = bell_draw(key_list[12], (D, D), D ** -0.5, 0.25)
    ffn_in = bell_draw(key_list[13], (D, FFN), D ** -0.5, 0.25)
    ffn_out = bell_draw(key_list[14], (FFN, D), FFN ** -0.5, 0.125)
    return {"inputs": inputs, "coverage": coverage, "encoded": encoded, "cross_list": cross_list, "gain_self": gain_self, "gain_cross": gain_cross, "gain_ffn": gain_ffn, "self_wq": self_wq, "self_wkv": self_wkv, "self_wo": self_wo, "cross_wq": cross_wq, "cross_wkv": cross_wkv, "cross_wo": cross_wo, "ffn_in": ffn_in, "ffn_out": ffn_out}


epsilon = 1e-05
mask_depth = 30.0

def layer_norm(values, gain_vec):
    widened = values.astype(jnp.float32)
    centre = widened - lax.optimization_barrier(jnp.mean(widened, axis=-1, keepdims=True))
    spread = lax.optimization_barrier(jnp.mean(centre * centre, axis=-1, keepdims=True))
    return (centre * lax.rsqrt(spread + epsilon) * gain_vec).astype(jnp.bfloat16)

def project(values, weight):
    return jnp.dot(values, weight, preferred_element_type=jnp.float32).astype(jnp.bfloat16)

def residual(base, update, weight):
    return (base.astype(jnp.float32) + jnp.dot(update, weight, preferred_element_type=jnp.float32)).astype(jnp.bfloat16)

def to_cuboids(grid_in, size_x, size_y):
    frame_count, row_count, col_count, channels = grid_in.shape
    split_grid = grid_in.reshape(frame_count, row_count // size_x, size_x, col_count // size_y, size_y, channels)
    return split_grid.transpose(1, 3, 0, 2, 4, 5).reshape(row_count // size_x, col_count // size_y, frame_count * size_x * size_y, channels)

def from_cuboids(blocks, frame_count, size_x, size_y):
    blocks_x, blocks_y, length, channels = blocks.shape
    split_grid = blocks.reshape(blocks_x, blocks_y, frame_count, size_x, size_y, channels)
    return split_grid.transpose(2, 0, 3, 1, 4, 5).reshape(frame_count, blocks_x * size_x, blocks_y * size_y, channels)

def cuboid_bias(cover, frame_count):
    blocks_x = cover.shape[0] // BX
    blocks_y = cover.shape[1] // BY
    tiles = cover.reshape(blocks_x, BX, blocks_y, BY).transpose(0, 2, 1, 3).reshape(blocks_x, blocks_y, 1, BX * BY)
    tiles = jnp.broadcast_to(tiles, (blocks_x, blocks_y, frame_count, BX * BY))
    return (tiles.reshape(blocks_x, blocks_y, frame_count * BX * BY) - 1.0) * mask_depth

def attend(queries, keys, values, bias, head_count):
    batches, query_count, features = queries.shape
    key_count = keys.shape[1]
    head_dim = features // head_count
    q_heads = queries.reshape(batches, query_count, head_count, head_dim).astype(jnp.float32)
    k_heads = keys.reshape(batches, key_count, head_count, head_dim).astype(jnp.float32)
    v_heads = values.reshape(batches, key_count, head_count, head_dim).astype(jnp.float32)
    scores = jnp.einsum('bqhd,bkhd->bhqk', q_heads, k_heads) * head_dim ** (-0.5)
    if bias is not None:
        scores = scores + bias[:, None, None, :]
    row_max = lax.optimization_barrier(jnp.max(scores, axis=-1, keepdims=True))
    weights = jnp.exp(scores - row_max)
    weights = (weights / lax.optimization_barrier(jnp.sum(weights, axis=-1, keepdims=True))).astype(jnp.bfloat16)
    mixed_out = jnp.einsum('bhqk,bkhd->bqhd', weights.astype(jnp.float32), v_heads)
    return mixed_out.reshape(batches, query_count, features).astype(jnp.bfloat16)

def reference(inputs, coverage, encoded, cross_list, gain_self, gain_cross, gain_ffn, self_wq, self_wkv, self_wo, cross_wq, cross_wkv, cross_wo, ffn_in, ffn_out):
    frame_count = inputs.shape[0]
    features = inputs.shape[-1]
    offset_rows = BX // 2
    normed = layer_norm(inputs, gain_self)
    queries = project(normed, self_wq)
    keyvals = project(normed, self_wkv)
    padding = ((0, 0), (offset_rows, offset_rows), (0, 0), (0, 0))
    q_blocks = to_cuboids(jnp.pad(queries, padding), BX, BY)
    kv_blocks = to_cuboids(jnp.pad(keyvals, padding), BX, BY)
    cover = jnp.pad(coverage.astype(jnp.float32), ((offset_rows, offset_rows), (0, 0)))
    bias_blocks = cuboid_bias(cover, frame_count)

    def self_column(columns_in):
        q_col, kv_col, bias_col = columns_in
        return attend(q_col, kv_col[..., :features], kv_col[..., features:], bias_col, HEADS)
    attended = lax.map(self_column, (q_blocks, kv_blocks, bias_blocks))
    attended = from_cuboids(attended, frame_count, BX, BY)[:, offset_rows:offset_rows + NX]
    first = residual(inputs, attended, self_wo)
    normed = layer_norm(first, gain_cross)
    cross_blocks = to_cuboids(project(normed, cross_wq), BX, BY)
    memory = project(encoded, cross_wkv).reshape(-1, encoded.shape[2], 2 * features)

    def cross_column(columns_in):
        q_col, cuboid_lists = columns_in
        chosen = memory[cuboid_lists].reshape(cuboid_lists.shape[0], -1, 2 * features)
        return attend(q_col, chosen[..., :features], chosen[..., features:], None, HEADS)
    attended = from_cuboids(lax.map(cross_column, (cross_blocks, cross_list)), frame_count, BX, BY)
    second = residual(first, attended, cross_wo)
    normed = layer_norm(second, gain_ffn)
    hidden = jax.nn.gelu(jnp.dot(normed, ffn_in, preferred_element_type=jnp.float32)).astype(jnp.bfloat16)
    return residual(second, hidden, ffn_out)
```

```python
import math

import jax
import jax.numpy as jnp
from jax import lax
from jax.experimental import pallas as pl
from jax.experimental.pallas import tpu as pltpu
from jax.sharding import PartitionSpec as P

HEADS = 8
BX = 8
BY = 8
HALF = BX // 2
LOG2E = math.log2(math.e)

epsilon = 1e-05
mask_depth = 30.0

F32 = jnp.float32
BF16 = jnp.bfloat16


def dot(a, b):
    return jnp.dot(a, b, preferred_element_type=F32)


def dot_nt(a, b):
    return lax.dot_general(a, b, (((1,), (1,)), ((), ())), preferred_element_type=F32)


def layer_norm(widened, gain_vec):
    centre = widened - jnp.mean(widened, axis=-1, keepdims=True)
    spread = jnp.mean(centre * centre, axis=-1, keepdims=True)
    return centre * lax.rsqrt(spread + epsilon) * gain_vec


def gelu(v):
    inner = v * (v * v * (math.sqrt(2 / math.pi) * 0.044715) + math.sqrt(2 / math.pi))
    half = 0.5 * v
    return half * jnp.tanh(inner) + half


def granules(block):
    wide = block.astype(F32)
    frames, rows, cols, features = wide.shape
    return [
        wide[:, :, j * BY : (j + 1) * BY].reshape(frames * rows * BY, features)
        for j in range(cols // BY)
    ]


def attend(q, k, v, bias):
    count, features = q.shape
    keys = k.shape[0]
    lane = lax.broadcasted_iota(jnp.int32, (count, 128), 1)
    low = lane < 64
    ones = jnp.ones((keys, 128), BF16)
    zero = jnp.zeros((count, 128), BF16)
    outs = []
    for p in range(features // 128):
        cols = slice(p * 128, p * 128 + 128)
        qp = q[:, cols]
        both = jnp.concatenate([jnp.where(low, qp, zero), jnp.where(low, zero, qp)], axis=0)
        scores = dot_nt(both, k[:, cols])
        if bias is not None:
            scores = scores + bias
        top = jnp.max(scores, axis=-1, keepdims=True)
        weights = jnp.exp2(scores - top).astype(BF16)
        mixed = dot(weights, jnp.concatenate([v[:, cols], ones], axis=1))
        num = jnp.where(low, mixed[:count, :128], mixed[count:, :128])
        den = jnp.where(low, mixed[:count, 128:], mixed[count:, 128:])
        outs.append((num / den).astype(BF16))
    return jnp.concatenate(outs, axis=1)


def finish_self(base, mixed, wo_ref, gain_cross, cwq_ref, first_ref, cq_ref):
    first = (base + dot(mixed, wo_ref[...])).astype(BF16)
    first_ref[...] = first.reshape(first_ref.shape)
    normed = layer_norm(first.astype(F32), gain_cross).astype(BF16)
    scale = LOG2E / 8.0
    cq_ref[...] = (dot(normed, cwq_ref[...]) * scale).astype(BF16).reshape(cq_ref.shape)


def inner_kernel(
    xa_ref, xb_ref, bias_ref, gs_ref, gc_ref, wq_ref, wkv_ref, wo_ref, cwq_ref, first_ref, cq_ref
):
    i = pl.program_id(0)
    features = wq_ref.shape[0]
    ga = granules(xa_ref[...])
    gb = granules(xb_ref[...])
    base = jnp.concatenate(ga + gb, axis=0)
    rows = ga[0].shape[0]
    normed = layer_norm(base, gs_ref[...]).astype(BF16)
    q = (dot(normed, wq_ref[...]) * (LOG2E / 8.0)).astype(BF16)
    kv = dot(normed, wkv_ref[...]).astype(BF16)
    parts = [None] * 4
    for j in range(2):
        def pick(a):
            return jnp.concatenate(
                [a[j * rows : (j + 1) * rows], a[(2 + j) * rows : (3 + j) * rows]], axis=0
            )

        bias = jnp.concatenate([bias_ref[2 + 2 * i, j], bias_ref[3 + 2 * i, j]], axis=1)
        kvj = pick(kv)
        mixed = attend(pick(q), kvj[:, :features], kvj[:, features:], bias)
        parts[j] = mixed[:rows]
        parts[2 + j] = mixed[rows:]
    finish_self(
        base, jnp.concatenate(parts, axis=0), wo_ref, gc_ref[...], cwq_ref, first_ref, cq_ref
    )


def edge_kernel(
    meta_ref,
    x_ref,
    pa_ref,
    pb_ref,
    bias_ref,
    gs_ref,
    gc_ref,
    wq_ref,
    wkv_ref,
    wo_ref,
    cwq_ref,
    first_in,
    cq_in,
    first_ref,
    cq_ref,
):
    del first_in, cq_in
    i = pl.program_id(0)
    features = wq_ref.shape[0]
    strip = meta_ref[0]
    from_row = ((strip + i) % 2) == 1
    outside = jnp.where(i == 0, strip == 0, strip == meta_ref[3] - 1)
    halo_block = jnp.where(from_row, pa_ref[...], pb_ref[...]).reshape(x_ref.shape)
    gh = granules(halo_block)
    go = granules(x_ref[...])
    rows = go[0].shape[0]
    keep = jnp.where(outside, 0.0, 1.0)
    own = jnp.concatenate(go, axis=0)
    normed_own = layer_norm(own, gs_ref[...]).astype(BF16)
    normed_halo = (layer_norm(jnp.concatenate(gh, axis=0), gs_ref[...]) * keep).astype(BF16)
    q = (dot(normed_own, wq_ref[...]) * (LOG2E / 8.0)).astype(BF16)
    kv = dot(jnp.concatenate([normed_halo, normed_own], axis=0), wkv_ref[...]).astype(BF16)
    parts = []
    for j in range(2):
        bias = jnp.concatenate([bias_ref[7 * i, j], bias_ref[1 + 5 * i, j]], axis=1)
        kvj = jnp.concatenate(
            [kv[j * rows : (j + 1) * rows], kv[(2 + j) * rows : (3 + j) * rows]], axis=0
        )
        parts.append(
            attend(q[j * rows : (j + 1) * rows], kvj[:, :features], kvj[:, features:], bias)
        )
    finish_self(
        own, jnp.concatenate(parts, axis=0), wo_ref, gc_ref[...], cwq_ref, first_ref, cq_ref
    )


def cross_kernel(
    meta_ref,
    list_ref,
    fa_ref,
    fb_ref,
    qa_ref,
    qb_ref,
    mine_ref,
    other_ref,
    ckv_ref,
    cwo_ref,
    gf_ref,
    fin_ref,
    fout_ref,
    out_ref,
):
    k = pl.program_id(0)
    strip, side, core = meta_ref[0], meta_ref[1], meta_ref[2]
    features = cwo_ref.shape[0]
    rows = fa_ref.shape[2]

    def entry(j, l):
        e = list_ref[(k * 2 + j) * 4 + l]
        delta = e // 8 - strip
        column = e % 8
        e_side, e_core, sub = column // 4, (column // 2) % 2, column % 2
        toward_row = jnp.where(strip % 2 == 0, 1, -1)
        slot = jnp.where(delta == 0, 0, jnp.where(delta == toward_row, 2, 4))
        slot = slot + jnp.where(e_side == side, 0, 1)
        place = slot * 2 + sub
        return jnp.where(e_core == core, mine_ref[place], other_ref[place])

    mixed = []
    for j in range(2):
        chosen = jnp.concatenate([entry(j, l) for l in range(4)], axis=0)
        kv = dot(chosen, ckv_ref[...]).astype(BF16)
        q = jnp.concatenate([qa_ref[0, j], qb_ref[0, j]], axis=0)
        mixed.append(attend(q, kv[:, :features], kv[:, features:], None))
    mixed = jnp.concatenate(mixed, axis=0)
    first = jnp.concatenate([fa_ref[0, 0], fb_ref[0, 0], fa_ref[0, 1], fb_ref[0, 1]], axis=0)
    second = (first.astype(F32) + dot(mixed, cwo_ref[...])).astype(BF16).astype(F32)
    normed = layer_norm(second, gf_ref[...]).astype(BF16)
    total = second
    hidden_units = fin_ref.shape[1]
    step = 512
    for c in range(0, hidden_units, step):
        hidden = gelu(dot(normed, fin_ref[:, c : c + step])).astype(BF16)
        total = total + dot(hidden, fout_ref[c : c + step, :])
    frames = out_ref.shape[0]
    shaped = total.reshape(2, 2, frames, HALF, BY, features)
    cols = jnp.concatenate([shaped[0], shaped[1]], axis=3).astype(BF16)
    out_ref[:, :HALF] = cols[0]
    out_ref[:, HALF:] = cols[1]


def whole(shape):
    return pl.BlockSpec(shape, lambda *_: (0,) * len(shape), pipeline_mode=pl.Buffered(1))


def pairs(strips, target):
    out = []
    for s in range(strips):
        for h in range(2):
            for c in range(2):
                s2, h2, c2 = target(s, h, c)
                out.append((s * 4 + h * 2 + c, s2 * 4 + h2 * 2 + c2))
    return out


def shards(
    inputs,
    coverage,
    encoded,
    cross_list,
    gain_self,
    gain_cross,
    gain_ffn,
    self_wq,
    self_wkv,
    self_wo,
    cross_wq,
    cross_wkv,
    cross_wo,
    ffn_in,
    ffn_out,
):
    frames, row_count, col_count, features = inputs.shape
    strips = lax.axis_size("gx")
    strip = lax.axis_index("gx")
    place = lax.axis_index("gy")
    meta = jnp.stack([strip, place // 2, place % 2, strips]).astype(jnp.int32)

    def across(s):
        far = s + 1 if s % 2 else s - 1
        return far if 0 <= far < strips else s

    def send(array, target):
        return lax.ppermute(array, ("gx", "gy"), pairs(strips, target))

    halo_tokens = frames * HALF * col_count
    piece = encoded.reshape(-1, features)
    tail = inputs[:, row_count - HALF :].reshape(halo_tokens, features)
    head = inputs[:, :HALF].reshape(halo_tokens, features)
    even = strip % 2 == 0
    to_row = jnp.concatenate([jnp.where(even, tail, head), piece], axis=0)
    to_across = jnp.concatenate([jnp.where(even, head, tail), piece], axis=0)
    got_row = send(to_row, lambda s, h, c: (s ^ 1, h, c))
    got_across = send(to_across, lambda s, h, c: (across(s), h, c))
    got_side = send(piece, lambda s, h, c: (s, 1 - h, c))
    got_row_side = send(piece, lambda s, h, c: (s ^ 1, 1 - h, c))
    got_across_side = send(piece, lambda s, h, c: (across(s), 1 - h, c))

    cover = jnp.pad(coverage.astype(F32), ((HALF, HALF), (0, 0)))
    cover = lax.dynamic_slice_in_dim(cover, strip * row_count, row_count + 2 * HALF, 0)
    quads = cover.shape[0] // HALF
    bias = (cover - 1.0) * (mask_depth * LOG2E)
    bias = bias.reshape(quads, 1, HALF, col_count // BY, BY).transpose(0, 3, 1, 2, 4)
    bias = jnp.broadcast_to(bias, (quads, col_count // BY, frames, HALF, BY))
    bias = bias.reshape(quads, col_count // BY, 1, frames * HALF * BY)

    gs = gain_self.reshape(1, features)
    gc = gain_cross.reshape(1, features)
    gf = gain_ffn.reshape(1, features)
    rows = frames * HALF * BY
    hidden_units = ffn_in.shape[1]
    quad_block = (frames, HALF, col_count, features)
    state = jax.ShapeDtypeStruct((6, 2, rows, features), BF16)
    params = pltpu.CompilerParams(vmem_limit_bytes=48 << 20)
    small = [
        whole((quads, 2, 1, rows)),
        whole((1, features)),
        whole((1, features)),
        whole((features, features)),
        whole((features, 2 * features)),
        whole((features, features)),
        whole((features, features)),
    ]
    small_args = (bias, gs, gc, self_wq, self_wkv, self_wo, cross_wq)

    first, cq = pl.pallas_call(
        inner_kernel,
        grid=(2,),
        in_specs=[
            pl.BlockSpec(quad_block, lambda i: (0, 1 + 2 * i, 0, 0)),
            pl.BlockSpec(quad_block, lambda i: (0, 2 + 2 * i, 0, 0)),
            *small,
        ],
        out_specs=[pl.BlockSpec((2, 2, rows, features), lambda i: (i, 0, 0, 0))] * 2,
        out_shape=[state, state],
        compiler_params=params,
        cost_estimate=pl.CostEstimate(flops=10 << 30, bytes_accessed=8 << 20, transcendentals=0),
    )(inputs, inputs, *small_args)

    edge_blocks = [pl.BlockSpec((1, 2, rows, features), lambda i: (4 + i, 0, 0, 0))] * 2
    first, cq = pl.pallas_call(
        edge_kernel,
        grid=(2,),
        in_specs=[
            pl.BlockSpec(memory_space=pltpu.SMEM),
            pl.BlockSpec(quad_block, lambda i: (0, 5 * i, 0, 0)),
            whole((halo_tokens, features)),
            whole((halo_tokens, features)),
            *small,
            pl.BlockSpec(memory_space=pl.ANY),
            pl.BlockSpec(memory_space=pl.ANY),
        ],
        out_specs=edge_blocks,
        out_shape=[state, state],
        input_output_aliases={11: 0, 12: 1},
        compiler_params=params,
        cost_estimate=pl.CostEstimate(flops=6 << 30, bytes_accessed=8 << 20, transcendentals=0),
    )(meta, inputs, got_row, got_across, *small_args, first, cq)

    mine = jnp.concatenate(
        [
            piece,
            got_side,
            got_row[halo_tokens:],
            got_row_side,
            got_across[halo_tokens:],
            got_across_side,
        ],
        axis=0,
    )
    other = send(mine, lambda s, h, c: (s, h, 1 - c))
    tokens = encoded.shape[2]
    window = (mine.shape[0] // tokens, tokens, features)
    lower = pl.BlockSpec((1, 2, rows, features), lambda k: (jnp.where(k == 0, 4, 2 * k - 1), 0, 0, 0))
    upper = pl.BlockSpec((1, 2, rows, features), lambda k: (jnp.where(k == 2, 5, 2 * k), 0, 0, 0))
    return pl.pallas_call(
        cross_kernel,
        grid=(3,),
        in_specs=[
            pl.BlockSpec(memory_space=pltpu.SMEM),
            pl.BlockSpec(memory_space=pltpu.SMEM),
            lower,
            upper,
            lower,
            upper,
            whole(window),
            whole(window),
            whole((features, 2 * features)),
            whole((features, features)),
            whole((1, features)),
            whole((features, hidden_units)),
            whole((hidden_units, features)),
        ],
        out_specs=pl.BlockSpec((frames, BX, col_count, features), lambda k: (0, k, 0, 0)),
        out_shape=jax.ShapeDtypeStruct(inputs.shape, BF16),
        compiler_params=params,
        cost_estimate=pl.CostEstimate(flops=20 << 30, bytes_accessed=16 << 20, transcendentals=0),
    )(
        meta,
        cross_list.reshape(-1),
        first,
        first,
        cq,
        cq,
        mine.reshape(window),
        other.reshape(window),
        cross_wkv,
        cross_wo,
        gf,
        ffn_in,
        ffn_out,
    )


def solution(mesh):
    return jax.shard_map(
        shards,
        mesh=mesh,
        in_specs=(
            P(None, "gx", "gy", None),
            P(None, "gy"),
            P("gx", "gy", None, None),
            P("gx", "gy", None),
            P(),
            P(),
            P(),
            P(),
            P(),
            P(),
            P(),
            P(),
            P(),
            P(),
            P(),
        ),
        out_specs=P(None, "gx", "gy", None),
        check_vma=False,
    )
```

```python
import functools
import math

import jax
import jax.numpy as jnp
from jax import lax
from jax.experimental import pallas as pl
from jax.experimental.pallas import tpu as pltpu
from jax.sharding import PartitionSpec as P

HEADS = 8
BX = 8
BY = 8
HALF = BX // 2
LOG2E = math.log2(math.e)

epsilon = 1e-05
mask_depth = 30.0

F32 = jnp.float32
BF16 = jnp.bfloat16


def dot(a, b):
    return jnp.dot(a, b, preferred_element_type=F32)


def dot_nt(a, b):
    return lax.dot_general(a, b, (((1,), (1,)), ((), ())), preferred_element_type=F32)


def layer_norm(widened, gain_vec):
    centre = widened - jnp.mean(widened, axis=-1, keepdims=True)
    spread = jnp.mean(centre * centre, axis=-1, keepdims=True)
    return centre * lax.rsqrt(spread + epsilon) * gain_vec


def gelu(v):
    inner = v * (v * v * (math.sqrt(2 / math.pi) * 0.044715) + math.sqrt(2 / math.pi))
    half = 0.5 * v
    return half * jnp.tanh(inner) + half


def granules(block):
    wide = block.astype(F32)
    frames, rows, cols, features = wide.shape
    return [
        wide[:, :, j * BY : (j + 1) * BY].reshape(frames * rows * BY, features)
        for j in range(cols // BY)
    ]


def attend(q, k, v, bias):
    count, features = q.shape
    keys = k.shape[0]
    lane = lax.broadcasted_iota(jnp.int32, (count, 128), 1)
    low = lane < 64
    ones = jnp.ones((keys, 128), BF16)
    zero = jnp.zeros((count, 128), BF16)
    outs = []
    for p in range(features // 128):
        cols = slice(p * 128, p * 128 + 128)
        qp = q[:, cols]
        both = jnp.concatenate([jnp.where(low, qp, zero), jnp.where(low, zero, qp)], axis=0)
        scores = dot_nt(both, k[:, cols])
        if bias is not None:
            scores = scores + bias
        top = jnp.max(scores, axis=-1, keepdims=True)
        weights = jnp.exp2(scores - top).astype(BF16)
        mixed = dot(weights, jnp.concatenate([v[:, cols], ones], axis=1))
        num = jnp.where(low, mixed[:count, :128], mixed[count:, :128])
        den = jnp.where(low, mixed[:count, 128:], mixed[count:, 128:])
        outs.append((num / den).astype(BF16))
    return jnp.concatenate(outs, axis=1)


def position():
    place = lax.axis_index("gy")
    return lax.axis_index("gx"), place // 2, place % 2


def first_cell(strip, row_count, total, window):
    block = jnp.maximum(strip * row_count - HALF, 0) // 128
    return pl.multiple_of(jnp.minimum(block, (total - window) // 128) * 128, 128)


def bias_rows(cover_ref, first_row, quads):
    cols, cells = cover_ref.shape
    cover = cover_ref[...].astype(BF16)
    key = lax.broadcasted_iota(jnp.int32, (128, cells), 0)
    cell = lax.broadcasted_iota(jnp.int32, (128, cells), 1)
    same_row = (cell % HALF) == (key // BY) % HALF
    line = lax.broadcasted_iota(jnp.int32, (8, cells), 0)
    wanted = jnp.full((8, cells), -9, jnp.int32)
    for n, quad in enumerate(quads):
        wanted = jnp.where(line == n, quad, wanted)
    grid_row = lax.broadcasted_iota(jnp.int32, (8, cells), 1) + first_row
    member = jnp.where(grid_row // HALF == wanted, 1.0, 0.0).astype(BF16)
    spot = lax.broadcasted_iota(jnp.int32, (128, cols), 0)
    col = lax.broadcasted_iota(jnp.int32, (128, cols), 1)
    out = []
    for j in range(cols // BY):
        pick = jnp.where(col == j * BY + spot % BY, 1.0, 0.0).astype(BF16)
        spread = jnp.where(same_row, dot(pick, cover), 0.0).astype(BF16)
        out.append((dot_nt(member, spread) - 1.0) * (mask_depth * LOG2E))
    return out


def copies(sems, moves):
    made = [pltpu.make_async_copy(src, dst, sems.at[n]) for n, (src, dst) in enumerate(moves)]
    for copy in made:
        copy.start()
    return made


def self_kernel(inner, edge, handoff, *refs):
    refs = list(refs)

    def take(count):
        out = refs[:count]
        del refs[:count]
        return out

    x_hbm, cover_hbm, gs_ref, gc_ref, wq_hbm, wkv_hbm, wo_hbm, cwq_hbm = take(8)
    halo_ref = take(1)[0] if edge else None
    piece_hbm = take(1)[0] if handoff else None
    first_hbm, cq_hbm = take(2)
    send_hbm = take(1)[0] if handoff else None
    x_buf, cover_buf, wq_buf, wkv_buf, wo_buf, cwq_buf, first_buf, cq_buf = take(8)
    sems, out_sems = refs

    strip = position()[0]
    even = strip % 2 == 0
    strips = lax.axis_size("gx")
    frames, row_count, cols, features = x_hbm.shape
    per_strip = row_count // HALF
    above = even if edge == "row" else jnp.logical_not(even)
    own_row = jnp.where(above, row_count - HALF, 0)
    start = first_cell(strip, row_count, cover_hbm.shape[1], cover_buf.shape[1])
    inputs = []
    if inner is not None:
        lo = HALF + inner * BX
        inputs.append((x_hbm.at[:, lo : lo + BX], x_buf.at[:, :BX]))
    if edge:
        at = x_buf.shape[1] - HALF
        inputs.append((x_hbm.at[:, pl.ds(own_row, HALF)], x_buf.at[:, at:]))
    tokens_at = len(inputs)
    inputs += [
        (wkv_hbm, wkv_buf),
        (wq_hbm, wq_buf),
        (cover_hbm.at[:, pl.ds(start, cover_buf.shape[1])], cover_buf),
        (wo_hbm, wo_buf),
        (cwq_hbm, cwq_buf),
    ]
    if handoff:
        far_row = jnp.where(even, 0, row_count - HALF)
        inputs.append((x_hbm.at[:, pl.ds(far_row, HALF)], send_hbm.at[:frames]))
        inputs.append((piece_hbm, send_hbm.at[frames:]))
    moves = copies(sems, inputs)
    for move in moves[:tokens_at]:
        move.wait()

    parts, quads, cuboids = [], [], []
    base_quad = strip * per_strip
    if inner is not None:
        for t in range(2):
            parts += granules(x_buf[:, t * HALF : (t + 1) * HALF])
            quads.append(base_quad + 1 + 2 * inner + t)
        cuboids += [((j, 2 + j), (j, 2 + j), (0, 1), j) for j in range(2)]
    if edge:
        n = len(parts)
        parts += granules(x_buf[:, at:])
        quads.append(base_quad + jnp.where(above, per_strip - 1, 0))
    own = len(parts)
    rows = parts[0].shape[0]
    base = jnp.concatenate(parts, axis=0)
    gs = gs_ref[...]
    normed = layer_norm(base, gs).astype(BF16)
    every = normed
    if edge:
        halo = layer_norm(jnp.concatenate(granules(halo_ref[:frames]), axis=0), gs)
        outside = jnp.where(above, strip == strips - 1, strip == 0)
        halo = (halo * jnp.where(outside, 0.0, 1.0)).astype(BF16)
        every = jnp.concatenate([normed, halo], axis=0)
        quads.append(quads[-1] + jnp.where(above, 1, -1))
        q_at = len(quads) - 2
        cuboids += [((n + j, own + j), (n + j,), (q_at, q_at + 1), j) for j in range(2)]
    for move in moves[tokens_at : tokens_at + 5]:
        move.wait()
    bias = bias_rows(cover_buf, start, quads)
    kv = dot(every, wkv_buf[...]).astype(BF16)
    q = (dot(normed, wq_buf[...]) * (LOG2E / 8.0)).astype(BF16)

    def pick(a, which):
        return jnp.concatenate([a[n * rows : (n + 1) * rows] for n in which], axis=0)

    mixed = [None] * own
    for keys, queries, lines, j in cuboids:
        keep = jnp.concatenate([bias[j][n : n + 1] for n in lines], axis=1)
        kvj = pick(kv, keys)
        out = attend(pick(q, queries), kvj[:, :features], kvj[:, features:], keep)
        for n, g in enumerate(queries):
            mixed[g] = out[n * rows : (n + 1) * rows]
    first = (base + dot(jnp.concatenate(mixed, axis=0), wo_buf[...])).astype(BF16)
    first_buf[...] = first.reshape(first_buf.shape)
    first_copy = pltpu.make_async_copy(first_buf, first_hbm, out_sems.at[0])
    first_copy.start()
    normed = layer_norm(first.astype(F32), gc_ref[...]).astype(BF16)
    cq_buf[...] = (dot(normed, cwq_buf[...]) * (LOG2E / 8.0)).astype(BF16).reshape(cq_buf.shape)
    cq_copy = pltpu.make_async_copy(cq_buf, cq_hbm, out_sems.at[1])
    cq_copy.start()
    for move in moves[tokens_at + 5 :]:
        move.wait()
    first_copy.wait()
    cq_copy.wait()


def cross_kernel(
    states,
    list_ref, mine_ref, other_ref, ckv_hbm, cwo_hbm, gf_ref, fin_hbm, fout_hbm, *refs,
):
    first_hbm, cq_hbm, refs = refs[:states], refs[states : 2 * states], refs[2 * states :]
    out_hbm, first_buf, cq_buf, ckv_buf, cwo_buf, fin_buf, fout_buf, out_buf = refs[:8]
    sems, out_sems = refs[8:]
    strip, side, core = position()
    features = cwo_hbm.shape[0]

    def laid(arrays, buf):
        out, at = [], 0
        for a in arrays:
            out.append((a, buf.at[at : at + a.shape[0]]))
            at += a.shape[0]
        return out

    early = [(ckv_hbm, ckv_buf), *laid(cq_hbm, cq_buf)]
    late = [(cwo_hbm, cwo_buf), *laid(first_hbm, first_buf), (fin_hbm, fin_buf), (fout_hbm, fout_buf)]
    moves = copies(sems, early + late)
    toward_row = jnp.where(strip % 2 == 0, 1, -1)

    def entry(n):
        e = list_ref[n // 8, n // 4 % 2, n % 4]
        delta = e // 8 - strip
        column = e % 8
        e_side, e_core, sub = column // 4, (column // 2) % 2, column % 2
        slot = jnp.where(delta == 0, 0, jnp.where(delta == toward_row, 2, 4))
        slot = slot + jnp.where(e_side == side, 0, 1)
        at = slot * 2 + sub
        return jnp.where(e_core == core, mine_ref[at], other_ref[at])

    for move in moves[: len(early)]:
        move.wait()
    tiles = out_hbm.shape[1] // BX
    top = jnp.where(strip % 2 == 0, 4, 5)
    slots = [(9 - top, 0), (1, 2), (3, top)]
    mixed = []
    for k in range(tiles):
        for j in range(2):
            chosen = jnp.concatenate([entry((k * 2 + j) * 4 + l) for l in range(4)], axis=0)
            kv = dot(chosen, ckv_buf[...]).astype(BF16)
            q = jnp.concatenate([cq_buf[s, j] for s in slots[k]], axis=0)
            mixed.append(attend(q, kv[:, :features], kv[:, features:], None))
    for move in moves[len(early) :]:
        move.wait()
    outs = []
    hidden_units = fin_hbm.shape[1]
    step = 1024
    frames = out_buf.shape[0]
    for k in range(tiles):
        first = jnp.concatenate([first_buf[s, j] for j in range(2) for s in slots[k]], axis=0)
        both = jnp.concatenate(mixed[2 * k : 2 * k + 2], axis=0)
        second = (first.astype(F32) + dot(both, cwo_buf[...])).astype(BF16).astype(F32)
        normed = layer_norm(second, gf_ref[...]).astype(BF16)
        total = second
        for c in range(0, hidden_units, step):
            hidden = gelu(dot(normed, fin_buf[:, c : c + step])).astype(BF16)
            total = total + dot(hidden, fout_buf[c : c + step, :])
        shaped = total.reshape(2, 2, frames, HALF, BY, features)
        cols = jnp.concatenate([shaped[0], shaped[1]], axis=3).astype(BF16)
        out_buf[:, k * BX : k * BX + HALF] = cols[0]
        out_buf[:, k * BX + HALF : (k + 1) * BX] = cols[1]
        here = slice(k * BX, (k + 1) * BX)
        outs.append(pltpu.make_async_copy(out_buf.at[:, here], out_hbm.at[:, here], out_sems.at[k]))
        outs[-1].start()
    for copy in outs:
        copy.wait()


def pairs(strips, target):
    out = []
    for s in range(strips):
        for h in range(2):
            for c in range(2):
                s2, h2, c2 = target(s, h, c)
                out.append((s * 4 + h * 2 + c, s2 * 4 + h2 * 2 + c2))
    return out


ANY = pl.BlockSpec(memory_space=pl.ANY)
SCALARS = pl.BlockSpec(memory_space=pltpu.SMEM)
FULL = pl.BlockSpec(memory_space=pltpu.VMEM)
COVER_CELLS = 256


def call(kernel, kinds, out_shape, scratch, copies_in, copies_out, mflops, mbytes, limit):
    return pl.pallas_call(
        kernel,
        in_specs=kinds,
        out_specs=jax.tree.map(lambda _: ANY, out_shape),
        out_shape=out_shape,
        scratch_shapes=[
            *scratch,
            pltpu.SemaphoreType.DMA((copies_in,)),
            pltpu.SemaphoreType.DMA((copies_out,)),
        ],
        compiler_params=pltpu.CompilerParams(vmem_limit_bytes=limit << 20),
        cost_estimate=pl.CostEstimate(
            flops=mflops * 10**6, bytes_accessed=mbytes << 20, transcendentals=0
        ),
    )


def self_call(x, cover, weights, inner, edge, halo=None, piece=None):
    frames, row_count, cols, features = x.shape
    rows = frames * HALF * BY
    quads = (0 if inner is None else 2) + (1 if edge else 0)
    state = jax.ShapeDtypeStruct((quads, cols // BY, rows, features), BF16)
    held = pltpu.VMEM(state.shape, BF16)
    outs = [state, state]
    extra, kinds = [], []
    if edge:
        extra.append(halo)
        kinds.append(FULL)
    if piece is not None:
        extra.append(piece)
        kinds.append(ANY)
        outs.append(jax.ShapeDtypeStruct((frames + piece.shape[0], *piece.shape[1:]), BF16))
    return call(
        functools.partial(self_kernel, inner, edge, piece is not None),
        [ANY, ANY, FULL, FULL, ANY, ANY, ANY, ANY, *kinds],
        outs,
        [
            pltpu.VMEM((frames, quads * HALF, cols, features), BF16),
            pltpu.VMEM((cols, COVER_CELLS), jnp.int32),
            pltpu.VMEM((features, features), BF16),
            pltpu.VMEM((features, 2 * features), BF16),
            pltpu.VMEM((features, features), BF16),
            pltpu.VMEM((features, features), BF16),
            held,
            held,
        ],
        10,
        2,
        2500 * quads,
        6,
        24,
    )(x, cover, *weights, *extra)


def cross_call(listed, mine, other, ckv, cwo, gf, fin, fout, firsts, cqs, frames=4):
    columns, rows, features = firsts[0].shape[1:]
    quads = sum(a.shape[0] for a in firsts)
    held = pltpu.VMEM((quads, columns, rows, features), BF16)
    out = jax.ShapeDtypeStruct((frames, quads * HALF, columns * BY, features), BF16)
    count = 2 * len(firsts)
    return call(
        functools.partial(cross_kernel, len(firsts)),
        [SCALARS, FULL, FULL, ANY, ANY, FULL, ANY, ANY, *[ANY] * count],
        out,
        [
            held,
            held,
            pltpu.VMEM(ckv.shape, BF16),
            pltpu.VMEM(cwo.shape, BF16),
            pltpu.VMEM(fin.shape, BF16),
            pltpu.VMEM(fout.shape, BF16),
            pltpu.VMEM(out.shape, BF16),
        ],
        4 + count,
        3,
        15000,
        12,
        40,
    )(listed, mine, other, ckv, cwo, gf, fin, fout, *firsts, *cqs)


def shards(
    inputs,
    coverage,
    encoded,
    cross_list,
    gain_self,
    gain_cross,
    gain_ffn,
    self_wq,
    self_wkv,
    self_wo,
    cross_wq,
    cross_wkv,
    cross_wo,
    ffn_in,
    ffn_out,
):
    frames, row_count, col_count, features = inputs.shape
    strips = lax.axis_size("gx")
    even = lax.axis_index("gx") % 2 == 0

    def across(s):
        far = s + 1 if s % 2 else s - 1
        return far if 0 <= far < strips else s

    def send(array, target):
        return lax.ppermute(array, ("gx", "gy"), pairs(strips, target))

    def to_row(s, h, c):
        return (s ^ 1, h, c)

    def to_across(s, h, c):
        return (across(s), h, c)

    def to_side(s, h, c):
        return (s, 1 - h, c)

    def to_row_side(s, h, c):
        return (s ^ 1, 1 - h, c)

    def to_across_side(s, h, c):
        return (across(s), 1 - h, c)

    def to_core(s, h, c):
        return (s, h, 1 - c)

    columns, tokens = encoded.shape[1:3]
    piece = encoded.reshape(columns, HALF, tokens // HALF, features)
    cover = coverage.T
    weights = (
        gain_self.reshape(1, features),
        gain_cross.reshape(1, features),
        self_wq,
        self_wkv,
        self_wo,
        cross_wq,
    )
    barrier = lax.optimization_barrier

    near_row = jnp.where(even, row_count - HALF, 0)
    near = lax.dynamic_slice_in_dim(inputs, near_row, HALF, axis=1)
    got_row = send(jnp.concatenate([near, piece], axis=0), to_row)
    first_a, cq_a, to_far = self_call(inputs, cover, weights, 0, None, piece=piece)
    piece_b, first_a, cq_a = barrier((piece, first_a, cq_a))
    got_across = send(to_far, to_across)
    got_side = send(piece_b, to_side)
    got_row_side = send(piece_b, to_row_side)
    got_across_side = send(piece_b, to_across_side)
    first_b, cq_b = self_call(inputs, cover, weights, 1, "row", halo=got_row)
    first_b, cq_b, got_across, got_side, got_row_side, got_across_side = barrier(
        (first_b, cq_b, got_across, got_side, got_row_side, got_across_side)
    )
    pieces = [piece, got_side, got_row[frames:], got_row_side, got_across[frames:], got_across_side]
    mine = jnp.concatenate([p.reshape(columns, tokens, features) for p in pieces], axis=0)
    other = send(mine, to_core)
    first_c, cq_c = self_call(inputs, cover, weights, None, "across", halo=got_across)

    return cross_call(
        cross_list,
        mine,
        other,
        cross_wkv,
        cross_wo,
        gain_ffn.reshape(1, features),
        ffn_in,
        ffn_out,
        [first_a, first_b, first_c],
        [cq_a, cq_b, cq_c],
    )


def solution(mesh):
    return jax.shard_map(
        shards,
        mesh=mesh,
        in_specs=(
            P(None, "gx", "gy", None),
            P(None, "gy"),
            P("gx", "gy", None, None),
            P("gx", "gy", None),
            P(),
            P(),
            P(),
            P(),
            P(),
            P(),
            P(),
            P(),
            P(),
            P(),
            P(),
        ),
        out_specs=P(None, "gx", "gy", None),
        check_vma=False,
    )
```

```python
import functools
import math

import jax
import jax.numpy as jnp
from jax import lax
from jax.experimental import pallas as pl
from jax.experimental.pallas import tpu as pltpu
from jax.sharding import PartitionSpec as P

HEADS = 8
BX = 8
BY = 8
HALF = BX // 2
LOG2E = math.log2(math.e)

epsilon = 1e-05
mask_depth = 30.0

F32 = jnp.float32
BF16 = jnp.bfloat16


def dot(a, b):
    return jnp.dot(a, b, preferred_element_type=F32)


def dot_nt(a, b):
    return lax.dot_general(a, b, (((1,), (1,)), ((), ())), preferred_element_type=F32)


def layer_norm(widened, gain_vec):
    centre = widened - jnp.mean(widened, axis=-1, keepdims=True)
    spread = jnp.mean(centre * centre, axis=-1, keepdims=True)
    return centre * lax.rsqrt(spread + epsilon) * gain_vec


def gelu(v):
    inner = v * (v * v * (math.sqrt(2 / math.pi) * 0.044715) + math.sqrt(2 / math.pi))
    half = 0.5 * v
    return half * jnp.tanh(inner) + half


def granules(block):
    wide = block.astype(F32)
    frames, rows, cols, features = wide.shape
    return [
        wide[:, :, j * BY : (j + 1) * BY].reshape(frames * rows * BY, features)
        for j in range(cols // BY)
    ]


def attend(q, k, v, bias):
    count, features = q.shape
    keys = k.shape[0]
    lane = lax.broadcasted_iota(jnp.int32, (count, 128), 1)
    low = lane < 64
    ones = jnp.ones((keys, 128), BF16)
    zero = jnp.zeros((count, 128), BF16)
    outs = []
    for p in range(features // 128):
        cols = slice(p * 128, p * 128 + 128)
        qp = q[:, cols]
        both = jnp.concatenate([jnp.where(low, qp, zero), jnp.where(low, zero, qp)], axis=0)
        scores = dot_nt(both, k[:, cols])
        if bias is not None:
            scores = scores + bias
        top = jnp.max(scores, axis=-1, keepdims=True)
        weights = jnp.exp2(scores - top).astype(BF16)
        mixed = dot(weights, jnp.concatenate([v[:, cols], ones], axis=1))
        num = jnp.where(low, mixed[:count, :128], mixed[count:, :128])
        den = jnp.where(low, mixed[:count, 128:], mixed[count:, 128:])
        outs.append((num / den).astype(BF16))
    return jnp.concatenate(outs, axis=1)


def position():
    place = lax.axis_index("gy")
    return lax.axis_index("gx"), place // 2, place % 2


def first_cell(strip, row_count, total, window):
    block = jnp.maximum(strip * row_count - HALF, 0) // 128
    return pl.multiple_of(jnp.minimum(block, (total - window) // 128) * 128, 128)


def bias_rows(cover_ref, first_row, quads):
    cols, cells = cover_ref.shape
    cover = cover_ref[...].astype(BF16)
    key = lax.broadcasted_iota(jnp.int32, (128, cells), 0)
    cell = lax.broadcasted_iota(jnp.int32, (128, cells), 1)
    same_row = (cell % HALF) == (key // BY) % HALF
    line = lax.broadcasted_iota(jnp.int32, (8, cells), 0)
    wanted = jnp.full((8, cells), -9, jnp.int32)
    for n, quad in enumerate(quads):
        wanted = jnp.where(line == n, quad, wanted)
    grid_row = lax.broadcasted_iota(jnp.int32, (8, cells), 1) + first_row
    member = jnp.where(grid_row // HALF == wanted, 1.0, 0.0).astype(BF16)
    spot = lax.broadcasted_iota(jnp.int32, (128, cols), 0)
    col = lax.broadcasted_iota(jnp.int32, (128, cols), 1)
    out = []
    for j in range(cols // BY):
        pick = jnp.where(col == j * BY + spot % BY, 1.0, 0.0).astype(BF16)
        spread = jnp.where(same_row, dot(pick, cover), 0.0).astype(BF16)
        out.append((dot_nt(member, spread) - 1.0) * (mask_depth * LOG2E))
    return out


def copies(sems, moves):
    made = [pltpu.make_async_copy(src, dst, sems.at[n]) for n, (src, dst) in enumerate(moves)]
    for copy in made:
        copy.start()
    return made


def pack_kernel(x_hbm, piece_hbm, row_ref, across_ref, sems):
    even = position()[0] % 2 == 0
    frames, row_count = x_hbm.shape[:2]
    last = row_count - HALF
    moves = copies(
        sems,
        [
            (x_hbm.at[:, pl.ds(jnp.where(even, last, 0), HALF)], row_ref.at[:frames]),
            (piece_hbm, row_ref.at[frames:]),
            (x_hbm.at[:, pl.ds(jnp.where(even, 0, last), HALF)], across_ref.at[:frames]),
            (piece_hbm, across_ref.at[frames:]),
        ],
    )
    for move in moves:
        move.wait()


def shifted_attention(strip, cover_buf, start, quads, cuboids, parts, halo, gs, gc, wq, wkv, wo, cwq, moves=()):
    features = wq.shape[0]
    rows = parts[0].shape[0]
    base = jnp.concatenate(parts, axis=0)
    normed = layer_norm(base, gs).astype(BF16)
    every = normed if halo is None else jnp.concatenate([normed, halo], axis=0)
    for move in moves[:3]:
        move.wait()
    bias = bias_rows(cover_buf, start, quads)
    kv = dot(every, wkv[...]).astype(BF16)
    q = (dot(normed, wq[...]) * (LOG2E / 8.0)).astype(BF16)

    def pick(a, which):
        return jnp.concatenate([a[n * rows : (n + 1) * rows] for n in which], axis=0)

    mixed = [None] * len(parts)
    for keys, queries, lines, j in cuboids:
        keep = jnp.concatenate([bias[j][n : n + 1] for n in lines], axis=1)
        kvj = pick(kv, keys)
        out = attend(pick(q, queries), kvj[:, :features], kvj[:, features:], keep)
        for n, g in enumerate(queries):
            mixed[g] = out[n * rows : (n + 1) * rows]
    for move in moves[3:]:
        move.wait()
    first = (base + dot(jnp.concatenate(mixed, axis=0), wo[...])).astype(BF16)
    normed = layer_norm(first.astype(F32), gc).astype(BF16)
    return first, (dot(normed, cwq[...]) * (LOG2E / 8.0)).astype(BF16)


def inner_kernel(
    x_hbm, cover_hbm, gs_ref, gc_ref, wq_hbm, wkv_hbm, wo_hbm, cwq_hbm, ckv_hbm, cwo_hbm,
    first_ref, cq_ref, sides_ref, cover_ref, wq, wkv, wo, cwq, ckv, cwo,
    x_buf, sems,
):
    strip = position()[0]
    even = strip % 2 == 0
    row_count = x_hbm.shape[1]
    last = row_count - HALF
    start = first_cell(strip, row_count, cover_hbm.shape[1], cover_ref.shape[1])
    inner = x_buf.shape[1]
    moves = copies(
        sems,
        [
            (x_hbm.at[:, HALF:last], x_buf),
            (wkv_hbm, wkv),
            (cover_hbm.at[:, pl.ds(start, cover_ref.shape[1])], cover_ref),
            (wq_hbm, wq),
            (wo_hbm, wo),
            (cwq_hbm, cwq),
            (x_hbm.at[:, pl.ds(jnp.where(even, last, 0), HALF)], sides_ref.at[0]),
            (x_hbm.at[:, pl.ds(jnp.where(even, 0, last), HALF)], sides_ref.at[1]),
            (ckv_hbm, ckv),
            (cwo_hbm, cwo),
        ],
    )
    moves[0].wait()
    parts, quads, cuboids = [], [], []
    for t in range(inner // HALF):
        parts += granules(x_buf[:, t * HALF : (t + 1) * HALF])
        quads.append(strip * (row_count // HALF) + 1 + t)
    for c in range(inner // BX):
        for j in range(2):
            pair = (4 * c + j, 4 * c + 2 + j)
            cuboids.append((pair, pair, (2 * c, 2 * c + 1), j))
    first, cq = shifted_attention(
        strip,
        cover_ref,
        start,
        quads,
        cuboids,
        parts,
        None,
        gs_ref[...],
        gc_ref[...],
        wq,
        wkv,
        wo,
        cwq,
        moves[1:6],
    )
    first_ref[...] = first.reshape(first_ref.shape)
    cq_ref[...] = cq.reshape(cq_ref.shape)
    for move in moves[6:]:
        move.wait()


def edge_kernel(
    row_ref, across_ref, sides_ref, cover_ref, gs_ref, gc_ref, wq, wkv, wo, cwq, first_ref, cq_ref, *, per_strip, cells
):
    strip = position()[0]
    strips = lax.axis_size("gx")
    even = strip % 2 == 0
    frames = sides_ref.shape[1]
    start = first_cell(strip, per_strip * HALF, cells, cover_ref.shape[1])
    gs = gs_ref[...]
    parts, quads, cuboids, halos = [], [], [], []
    for n, halo_ref in enumerate((row_ref, across_ref)):
        above = even if n == 0 else jnp.logical_not(even)
        parts += granules(sides_ref[n])
        own = strip * per_strip + jnp.where(above, per_strip - 1, 0)
        quads += [own, own + jnp.where(above, 1, -1)]
        halo = layer_norm(jnp.concatenate(granules(halo_ref[:frames]), axis=0), gs)
        outside = jnp.where(above, strip == strips - 1, strip == 0)
        halos.append((halo * jnp.where(outside, 0.0, 1.0)).astype(BF16))
        for j in range(2):
            g = 2 * n + j
            cuboids.append(((g, 4 + g), (g,), (2 * n, 2 * n + 1), j))
    first, cq = shifted_attention(
        strip,
        cover_ref,
        start,
        quads,
        cuboids,
        parts,
        jnp.concatenate(halos, axis=0),
        gs,
        gc_ref[...],
        wq,
        wkv,
        wo,
        cwq,
    )
    first_ref[...] = first.reshape(first_ref.shape)
    cq_ref[...] = cq.reshape(cq_ref.shape)


def cross_kernel(states, list_ref, mine_ref, other_ref, ckv_ref, cwo_ref, gf_ref, fin_hbm, fout_hbm, *refs):
    first_refs, cq_refs, refs = refs[:states], refs[states : 2 * states], refs[2 * states :]
    out_hbm, first_buf, cq_buf, out_buf, fin_ref, fout_ref, sems, out_sems = refs
    moves = copies(sems, [(fin_hbm, fin_ref), (fout_hbm, fout_ref)])
    strip, side, core = position()
    features = cwo_ref.shape[0]

    def gather(arrays, buf):
        at = 0
        for a in arrays:
            buf[at : at + a.shape[0]] = a[...]
            at += a.shape[0]

    gather(first_refs, first_buf)
    gather(cq_refs, cq_buf)
    toward_row = jnp.where(strip % 2 == 0, 1, -1)

    def entry(n):
        e = list_ref[n // 8, n // 4 % 2, n % 4]
        delta = e // 8 - strip
        column = e % 8
        e_side, e_core, sub = column // 4, (column // 2) % 2, column % 2
        slot = jnp.where(delta == 0, 0, jnp.where(delta == toward_row, 2, 4))
        slot = slot + jnp.where(e_side == side, 0, 1)
        at = slot * 2 + sub
        return jnp.where(e_core == core, mine_ref[at], other_ref[at])

    tiles = out_hbm.shape[1] // BX
    top = jnp.where(strip % 2 == 0, 4, 5)
    slots = [(9 - top, 0), (1, 2), (3, top)]
    kvs = []
    for n in range(2 * tiles):
        chosen = jnp.concatenate([entry(n * 4 + l) for l in range(4)], axis=0)
        kvs.append(dot(chosen, ckv_ref[...]).astype(BF16))
    mixed = []
    for k in range(tiles):
        for j in range(2):
            kv = kvs[2 * k + j]
            q = jnp.concatenate([cq_buf[s, j] for s in slots[k]], axis=0)
            mixed.append(attend(q, kv[:, :features], kv[:, features:], None))
    for move in moves:
        move.wait()
    outs = []
    hidden_units = fin_ref.shape[1]
    step = 2048
    frames = out_buf.shape[0]
    for k in range(tiles):
        first = jnp.concatenate([first_buf[s, j] for j in range(2) for s in slots[k]], axis=0)
        both = jnp.concatenate(mixed[2 * k : 2 * k + 2], axis=0)
        second = (first.astype(F32) + dot(both, cwo_ref[...])).astype(BF16).astype(F32)
        normed = layer_norm(second, gf_ref[...]).astype(BF16)
        total = second
        for c in range(0, hidden_units, step):
            hidden = gelu(dot(normed, fin_ref[:, c : c + step])).astype(BF16)
            total = total + dot(hidden, fout_ref[c : c + step, :])
        shaped = total.reshape(2, 2, frames, HALF, BY, features)
        cols = jnp.concatenate([shaped[0], shaped[1]], axis=3).astype(BF16)
        out_buf[:, k * BX : k * BX + HALF] = cols[0]
        out_buf[:, k * BX + HALF : (k + 1) * BX] = cols[1]
        here = slice(k * BX, (k + 1) * BX)
        outs.append(pltpu.make_async_copy(out_buf.at[:, here], out_hbm.at[:, here], out_sems.at[k]))
        outs[-1].start()
    for copy in outs:
        copy.wait()


def pairs(strips, target):
    out = []
    for s in range(strips):
        for h in range(2):
            for c in range(2):
                s2, h2, c2 = target(s, h, c)
                out.append((s * 4 + h * 2 + c, s2 * 4 + h2 * 2 + c2))
    return out


ANY = pl.BlockSpec(memory_space=pl.ANY)
HBM = pl.BlockSpec(memory_space=pltpu.HBM)
SCALARS = pl.BlockSpec(memory_space=pltpu.SMEM)
FULL = pl.BlockSpec(memory_space=pltpu.VMEM)
COVER_CELLS = 256


def call(kernel, kinds, out_shape, scratch, sems, out_kind, mflops, mbytes, limit):
    return pl.pallas_call(
        kernel,
        in_specs=kinds,
        out_specs=jax.tree.map(lambda _: out_kind, out_shape),
        out_shape=out_shape,
        scratch_shapes=[*scratch, *sems],
        compiler_params=pltpu.CompilerParams(vmem_limit_bytes=limit << 20),
        cost_estimate=pl.CostEstimate(
            flops=mflops * 10**6, bytes_accessed=mbytes << 20, transcendentals=0
        ),
    )


def pack_call(x, piece):
    frames, _, cols, features = x.shape
    out = jax.ShapeDtypeStruct((frames + piece.shape[0], HALF, cols, features), BF16)
    return pl.pallas_call(
        pack_kernel,
        in_specs=[ANY, ANY],
        out_specs=[FULL, FULL],
        out_shape=[out, out],
        scratch_shapes=[pltpu.SemaphoreType.DMA((4,))],
        cost_estimate=pl.CostEstimate(flops=0, bytes_accessed=2 << 20, transcendentals=0),
    )(x, piece)


def inner_call(x, cover, gs, gc, weights):
    frames, row_count, cols, features = x.shape
    rows = frames * HALF * BY
    quads = row_count // HALF - 2
    state = jax.ShapeDtypeStruct((quads, cols // BY, rows, features), BF16)
    return call(
        inner_kernel,
        [HBM, HBM, FULL, FULL, *[HBM] * len(weights)],
        [
            state,
            state,
            jax.ShapeDtypeStruct((2, frames, HALF, cols, features), BF16),
            jax.ShapeDtypeStruct((cols, COVER_CELLS), jnp.int32),
            *[jax.ShapeDtypeStruct(w.shape, w.dtype) for w in weights],
        ],
        [pltpu.VMEM((frames, row_count - BX, cols, features), BF16)],
        [pltpu.SemaphoreType.DMA((10,))],
        FULL,
        8000,
        10,
        53,
    )(x, cover, gs, gc, *weights)


def edge_call(row, across, sides, cover_part, gs, gc, wq, wkv, wo, cwq, row_count, cells):
    _, frames, _, cols, features = sides.shape
    rows = frames * HALF * BY
    state = jax.ShapeDtypeStruct((2, cols // BY, rows, features), BF16)
    return call(
        functools.partial(edge_kernel, per_strip=row_count // HALF, cells=cells),
        [FULL] * 10,
        [state, state],
        [],
        [],
        FULL,
        6000,
        4,
        28,
    )(row, across, sides, cover_part, gs, gc, wq, wkv, wo, cwq)


def cross_call(listed, mine, other, ckv, cwo, gf, fin, fout, firsts, cqs, frames=4):
    columns, rows, features = firsts[0].shape[1:]
    quads = sum(a.shape[0] for a in firsts)
    held = pltpu.VMEM((quads, columns, rows, features), BF16)
    out = jax.ShapeDtypeStruct((frames, quads * HALF, columns * BY, features), BF16)
    count = 2 * len(firsts)
    return call(
        functools.partial(cross_kernel, len(firsts)),
        [SCALARS, *[FULL] * 5, HBM, HBM, *[FULL] * count],
        out,
        [
            held,
            held,
            pltpu.VMEM(out.shape, BF16),
            pltpu.VMEM(fin.shape, BF16),
            pltpu.VMEM(fout.shape, BF16),
        ],
        [pltpu.SemaphoreType.DMA((2,)), pltpu.SemaphoreType.DMA((3,))],
        ANY,
        15000,
        12,
        40,
    )(listed, mine, other, ckv, cwo, gf, fin, fout, *firsts, *cqs)


def shards(
    inputs,
    coverage,
    encoded,
    cross_list,
    gain_self,
    gain_cross,
    gain_ffn,
    self_wq,
    self_wkv,
    self_wo,
    cross_wq,
    cross_wkv,
    cross_wo,
    ffn_in,
    ffn_out,
):
    frames, row_count, col_count, features = inputs.shape
    strips = lax.axis_size("gx")
    even = lax.axis_index("gx") % 2 == 0

    def across(s):
        far = s + 1 if s % 2 else s - 1
        return far if 0 <= far < strips else s

    def send(array, target):
        return lax.ppermute(array, ("gx", "gy"), pairs(strips, target))

    def to_row(s, h, c):
        return (s ^ 1, h, c)

    def to_across(s, h, c):
        return (across(s), h, c)

    def to_side(s, h, c):
        return (s, 1 - h, c)

    def to_row_side(s, h, c):
        return (s ^ 1, 1 - h, c)

    def to_across_side(s, h, c):
        return (across(s), 1 - h, c)

    def to_core(s, h, c):
        return (s, h, 1 - c)

    columns, tokens = encoded.shape[1:3]
    piece = encoded.reshape(columns, HALF, tokens // HALF, features)
    cover = coverage.T
    gs = gain_self.reshape(1, features)
    gc = gain_cross.reshape(1, features)
    barrier = lax.optimization_barrier

    to_near, to_far = pack_call(inputs, piece)
    got_row = send(to_near, to_row)
    got_across = send(to_far, to_across)
    got_side = send(piece, to_side)
    got_row_side = send(piece, to_row_side)
    got_across_side = send(piece, to_across_side)
    first_a, cq_a, sides, cover_part, *weights = inner_call(
        inputs,
        cover,
        gs,
        gc,
        (self_wq, self_wkv, self_wo, cross_wq, cross_wkv, cross_wo),
    )
    first_a, cq_a, got_row, got_across, got_side, got_row_side, got_across_side = barrier(
        (first_a, cq_a, got_row, got_across, got_side, got_row_side, got_across_side)
    )
    pieces = [piece, got_side, got_row[frames:], got_row_side, got_across[frames:], got_across_side]
    mine = jnp.concatenate([p.reshape(columns, tokens, features) for p in pieces], axis=0)
    other = send(mine, to_core)
    first_b, cq_b = edge_call(
        got_row, got_across, sides, cover_part, gs, gc, *weights[:4], row_count, cover.shape[1]
    )
    return cross_call(
        cross_list,
        mine,
        other,
        *weights[4:6],
        gain_ffn.reshape(1, features),
        ffn_in,
        ffn_out,
        [first_a, first_b],
        [cq_a, cq_b],
    )


def solution(mesh):
    return jax.shard_map(
        shards,
        mesh=mesh,
        in_specs=(
            P(None, "gx", "gy", None),
            P(None, "gy"),
            P("gx", "gy", None, None),
            P("gx", "gy", None),
            P(),
            P(),
            P(),
            P(),
            P(),
            P(),
            P(),
            P(),
            P(),
            P(),
            P(),
        ),
        out_specs=P(None, "gx", "gy", None),
        check_vma=False,
    )
```

```python
import functools
import math

import jax
import jax.numpy as jnp
from jax import lax
from jax.experimental import pallas as pl
from jax.experimental.pallas import tpu as pltpu
from jax.sharding import PartitionSpec as P

HEADS = 8
BX = 8
BY = 8
HALF = BX // 2
LOG2E = math.log2(math.e)

epsilon = 1e-05
mask_depth = 30.0

F32 = jnp.float32
BF16 = jnp.bfloat16


def dot(a, b):
    return jnp.dot(a, b, preferred_element_type=F32)


def dot_nt(a, b):
    return lax.dot_general(a, b, (((1,), (1,)), ((), ())), preferred_element_type=F32)


def layer_norm(widened, gain_vec):
    centre = widened - jnp.mean(widened, axis=-1, keepdims=True)
    spread = jnp.mean(centre * centre, axis=-1, keepdims=True)
    return centre * lax.rsqrt(spread + epsilon) * gain_vec


def gelu(v):
    inner = v * (v * v * (math.sqrt(2 / math.pi) * 0.044715) + math.sqrt(2 / math.pi))
    half = 0.5 * v
    return half * jnp.tanh(inner) + half


def granules(block):
    wide = block.astype(F32)
    frames, rows, cols, features = wide.shape
    return [
        wide[:, :, j * BY : (j + 1) * BY].reshape(frames * rows * BY, features)
        for j in range(cols // BY)
    ]


def attend(q, k, v, bias):
    count, features = q.shape
    keys = k.shape[0]
    lane = lax.broadcasted_iota(jnp.int32, (count, 128), 1)
    low = lane < 64
    ones = jnp.ones((keys, 128), BF16)
    zero = jnp.zeros((count, 128), BF16)
    outs = []
    for p in range(features // 128):
        cols = slice(p * 128, p * 128 + 128)
        qp = q[:, cols]
        both = jnp.concatenate([jnp.where(low, qp, zero), jnp.where(low, zero, qp)], axis=0)
        scores = dot_nt(both, k[:, cols])
        if bias is not None:
            scores = scores + bias
        top = jnp.max(scores, axis=-1, keepdims=True)
        weights = jnp.exp2(scores - top).astype(BF16)
        mixed = dot(weights, jnp.concatenate([v[:, cols], ones], axis=1))
        num = jnp.where(low, mixed[:count, :128], mixed[count:, :128])
        den = jnp.where(low, mixed[:count, 128:], mixed[count:, 128:])
        outs.append((num / den).astype(BF16))
    return jnp.concatenate(outs, axis=1)


def position():
    place = lax.axis_index("gy")
    return lax.axis_index("gx"), place // 2, place % 2


def first_cell(strip, row_count, total, window):
    block = jnp.maximum(strip * row_count - HALF, 0) // 128
    return pl.multiple_of(jnp.minimum(block, (total - window) // 128) * 128, 128)


def bias_rows(cover_ref, first_row, quads):
    cols, cells = cover_ref.shape
    cover = cover_ref[...].astype(BF16)
    key = lax.broadcasted_iota(jnp.int32, (128, cells), 0)
    cell = lax.broadcasted_iota(jnp.int32, (128, cells), 1)
    same_row = (cell % HALF) == (key // BY) % HALF
    line = lax.broadcasted_iota(jnp.int32, (8, cells), 0)
    wanted = jnp.full((8, cells), -9, jnp.int32)
    for n, quad in enumerate(quads):
        wanted = jnp.where(line == n, quad, wanted)
    grid_row = lax.broadcasted_iota(jnp.int32, (8, cells), 1) + first_row
    member = jnp.where(grid_row // HALF == wanted, 1.0, 0.0).astype(BF16)
    spot = lax.broadcasted_iota(jnp.int32, (128, cols), 0)
    col = lax.broadcasted_iota(jnp.int32, (128, cols), 1)
    out = []
    for j in range(cols // BY):
        pick = jnp.where(col == j * BY + spot % BY, 1.0, 0.0).astype(BF16)
        spread = jnp.where(same_row, dot(pick, cover), 0.0).astype(BF16)
        out.append((dot_nt(member, spread) - 1.0) * (mask_depth * LOG2E))
    return out


def copies(sems, moves):
    made = [pltpu.make_async_copy(src, dst, sems.at[n]) for n, (src, dst) in enumerate(moves)]
    for copy in made:
        copy.start()
    return made


def pack_kernel(x_hbm, piece_hbm, row_ref, across_ref, sems):
    even = position()[0] % 2 == 0
    frames, row_count = x_hbm.shape[:2]
    last = row_count - HALF
    moves = copies(
        sems,
        [
            (x_hbm.at[:, pl.ds(jnp.where(even, last, 0), HALF)], row_ref.at[:frames]),
            (piece_hbm, row_ref.at[frames:]),
            (x_hbm.at[:, pl.ds(jnp.where(even, 0, last), HALF)], across_ref.at[:frames]),
            (piece_hbm, across_ref.at[frames:]),
        ],
    )
    for move in moves:
        move.wait()


def shifted_attention(strip, cover_buf, start, quads, cuboids, parts, halo, gs, gc, wq, wkv, wo, cwq, moves=()):
    features = wq.shape[0]
    rows = parts[0].shape[0]
    base = jnp.concatenate(parts, axis=0)
    normed = layer_norm(base, gs).astype(BF16)
    every = normed if halo is None else jnp.concatenate([normed, halo], axis=0)
    for move in moves[:3]:
        move.wait()
    bias = bias_rows(cover_buf, start, quads)
    kv = dot(every, wkv[...]).astype(BF16)
    q = (dot(normed, wq[...]) * (LOG2E / 8.0)).astype(BF16)

    def pick(a, which):
        return jnp.concatenate([a[n * rows : (n + 1) * rows] for n in which], axis=0)

    mixed = [None] * len(parts)
    for keys, queries, lines, j in cuboids:
        keep = jnp.concatenate([bias[j][n : n + 1] for n in lines], axis=1)
        kvj = pick(kv, keys)
        out = attend(pick(q, queries), kvj[:, :features], kvj[:, features:], keep)
        for n, g in enumerate(queries):
            mixed[g] = out[n * rows : (n + 1) * rows]
    for move in moves[3:]:
        move.wait()
    first = (base + dot(jnp.concatenate(mixed, axis=0), wo[...])).astype(BF16)
    normed = layer_norm(first.astype(F32), gc).astype(BF16)
    return first, (dot(normed, cwq[...]) * (LOG2E / 8.0)).astype(BF16)


def inner_kernel(
    x_hbm, cover_hbm, gs_ref, gc_ref, wq_hbm, wkv_hbm, wo_hbm, cwq_hbm,
    first_ref, cq_ref,
    x_buf, cover_ref, wq, wkv, wo, cwq, sems,
):
    strip = position()[0]
    row_count = x_hbm.shape[1]
    last = row_count - HALF
    start = first_cell(strip, row_count, cover_hbm.shape[1], cover_ref.shape[1])
    inner = x_buf.shape[1]
    moves = copies(
        sems,
        [
            (x_hbm.at[:, HALF:last], x_buf),
            (wkv_hbm, wkv),
            (cover_hbm.at[:, pl.ds(start, cover_ref.shape[1])], cover_ref),
            (wq_hbm, wq),
            (wo_hbm, wo),
            (cwq_hbm, cwq),
        ],
    )
    moves[0].wait()
    parts, quads, cuboids = [], [], []
    for t in range(inner // HALF):
        parts += granules(x_buf[:, t * HALF : (t + 1) * HALF])
        quads.append(strip * (row_count // HALF) + 1 + t)
    for c in range(inner // BX):
        for j in range(2):
            pair = (4 * c + j, 4 * c + 2 + j)
            cuboids.append((pair, pair, (2 * c, 2 * c + 1), j))
    first, cq = shifted_attention(
        strip,
        cover_ref,
        start,
        quads,
        cuboids,
        parts,
        None,
        gs_ref[...],
        gc_ref[...],
        wq,
        wkv,
        wo,
        cwq,
        moves[1:6],
    )
    first_ref[...] = first.reshape(first_ref.shape)
    cq_ref[...] = cq.reshape(cq_ref.shape)
    for move in moves[6:]:
        move.wait()


def edge_kernel(
    row_ref, across_ref, x_hbm, cover_hbm, gs_ref, gc_ref, wq_hbm, wkv_hbm, wo_hbm, cwq_hbm,
    first_ref, cq_ref, sides_ref, cover_ref, wq, wkv, wo, cwq, sems,
):
    strip = position()[0]
    row_count = x_hbm.shape[1]
    per_strip = row_count // HALF
    strips = lax.axis_size("gx")
    even = strip % 2 == 0
    frames = sides_ref.shape[1]
    start = first_cell(strip, row_count, cover_hbm.shape[1], cover_ref.shape[1])
    last = row_count - HALF
    moves = copies(
        sems,
        [
            (x_hbm.at[:, pl.ds(jnp.where(even, last, 0), HALF)], sides_ref.at[0]),
            (x_hbm.at[:, pl.ds(jnp.where(even, 0, last), HALF)], sides_ref.at[1]),
            (cover_hbm.at[:, pl.ds(start, cover_ref.shape[1])], cover_ref),
            (wkv_hbm, wkv),
            (wq_hbm, wq),
            (wo_hbm, wo),
            (cwq_hbm, cwq),
        ],
    )
    for move in moves[:2]:
        move.wait()
    gs = gs_ref[...]
    parts, quads, cuboids, halos = [], [], [], []
    for n, halo_ref in enumerate((row_ref, across_ref)):
        above = even if n == 0 else jnp.logical_not(even)
        parts += granules(sides_ref[n])
        own = strip * per_strip + jnp.where(above, per_strip - 1, 0)
        quads += [own, own + jnp.where(above, 1, -1)]
        halo = layer_norm(jnp.concatenate(granules(halo_ref[:frames]), axis=0), gs)
        outside = jnp.where(above, strip == strips - 1, strip == 0)
        halos.append((halo * jnp.where(outside, 0.0, 1.0)).astype(BF16))
        for j in range(2):
            g = 2 * n + j
            cuboids.append(((g, 4 + g), (g,), (2 * n, 2 * n + 1), j))
    first, cq = shifted_attention(
        strip,
        cover_ref,
        start,
        quads,
        cuboids,
        parts,
        jnp.concatenate(halos, axis=0),
        gs,
        gc_ref[...],
        wq,
        wkv,
        wo,
        cwq,
        moves[2:],
    )
    first_ref[...] = first.reshape(first_ref.shape)
    cq_ref[...] = cq.reshape(cq_ref.shape)


def cross_kernel(states, list_ref, w0_ref, w1_ref, w2_ref, w3_ref, ckv_ref, cwo_ref, gf_ref, fin_hbm, fout_hbm, *refs):
    first_refs, cq_refs, refs = refs[:states], refs[states : 2 * states], refs[2 * states :]
    out_hbm, window, out_buf, fin_ref, fout_ref, sems, out_sems = refs
    moves = copies(sems, [(fin_hbm, fin_ref), (fout_hbm, fout_ref)])
    strip, side, core = position()
    features = cwo_ref.shape[0]
    tiles = out_hbm.shape[1] // BX

    def granule(refs, quad, j):
        inner, edges = refs
        at_top = strip % 2 == 0
        if quad == 0:
            return edges[jnp.where(at_top, 1, 0), j]
        if quad == 2 * tiles - 1:
            return edges[jnp.where(at_top, 0, 1), j]
        return inner[quad - 1, j]

    at = 0
    for part in (w0_ref, w1_ref, w2_ref, w3_ref):
        window[at : at + part.shape[0]] = part[...]
        at += part.shape[0]
    toward_row = jnp.where(strip % 2 == 0, 1, -1)

    def entry(n):
        e = list_ref[n // 8, n // 4 % 2, n % 4]
        delta = e // 8 - strip
        column = e % 8
        e_side, e_core, sub = column // 4, (column // 2) % 2, column % 2
        same = e_side == side
        near = jnp.where(delta == toward_row, 0, 1)
        slot = jnp.where(same, 2, 4) + near
        slot = jnp.where(delta == 0, jnp.where(same, 0, 1), slot)
        half = window.shape[0] // 2
        return window[jnp.where(e_core == core, 0, half) + slot * 2 + sub]

    kvs = []
    for n in range(2 * tiles):
        chosen = jnp.concatenate([entry(n * 4 + l) for l in range(4)], axis=0)
        kvs.append(dot(chosen, ckv_ref[...]).astype(BF16))
    mixed = []
    for k in range(tiles):
        for j in range(2):
            kv = kvs[2 * k + j]
            q = jnp.concatenate([granule(cq_refs, 2 * k + t, j) for t in range(2)], axis=0)
            mixed.append(attend(q, kv[:, :features], kv[:, features:], None))
    for move in moves:
        move.wait()
    outs = []
    hidden_units = fin_ref.shape[1]
    step = 2048
    frames = out_buf.shape[0]
    for k in range(tiles):
        first = jnp.concatenate(
            [granule(first_refs, 2 * k + t, j) for j in range(2) for t in range(2)], axis=0
        )
        both = jnp.concatenate(mixed[2 * k : 2 * k + 2], axis=0)
        second = (first.astype(F32) + dot(both, cwo_ref[...])).astype(BF16).astype(F32)
        normed = layer_norm(second, gf_ref[...]).astype(BF16)
        total = second
        for c in range(0, hidden_units, step):
            hidden = gelu(dot(normed, fin_ref[:, c : c + step])).astype(BF16)
            total = total + dot(hidden, fout_ref[c : c + step, :])
        shaped = total.reshape(2, 2, frames, HALF, BY, features)
        cols = jnp.concatenate([shaped[0], shaped[1]], axis=3).astype(BF16)
        out_buf[:, k * BX : k * BX + HALF] = cols[0]
        out_buf[:, k * BX + HALF : (k + 1) * BX] = cols[1]
        here = slice(k * BX, (k + 1) * BX)
        outs.append(pltpu.make_async_copy(out_buf.at[:, here], out_hbm.at[:, here], out_sems.at[k]))
        outs[-1].start()
    for copy in outs:
        copy.wait()


def pairs(strips, target):
    out = []
    for s in range(strips):
        for h in range(2):
            for c in range(2):
                s2, h2, c2 = target(s, h, c)
                out.append((s * 4 + h * 2 + c, s2 * 4 + h2 * 2 + c2))
    return out


ANY = pl.BlockSpec(memory_space=pl.ANY)
HBM = pl.BlockSpec(memory_space=pltpu.HBM)
SCALARS = pl.BlockSpec(memory_space=pltpu.SMEM)
FULL = pl.BlockSpec(memory_space=pltpu.VMEM)
COVER_CELLS = 256


def call(kernel, kinds, out_shape, scratch, sems, out_kind, mflops, mbytes, limit):
    return pl.pallas_call(
        kernel,
        in_specs=kinds,
        out_specs=jax.tree.map(lambda _: out_kind, out_shape),
        out_shape=out_shape,
        scratch_shapes=[*scratch, *sems],
        compiler_params=pltpu.CompilerParams(vmem_limit_bytes=limit << 20),
        cost_estimate=pl.CostEstimate(
            flops=mflops * 10**6, bytes_accessed=mbytes << 20, transcendentals=0
        ),
    )


def pack_call(x, piece):
    frames, _, cols, features = x.shape
    out = jax.ShapeDtypeStruct((frames + piece.shape[0], HALF, cols, features), BF16)
    return pl.pallas_call(
        pack_kernel,
        in_specs=[ANY, ANY],
        out_specs=[FULL, FULL],
        out_shape=[out, out],
        scratch_shapes=[pltpu.SemaphoreType.DMA((4,))],
        cost_estimate=pl.CostEstimate(flops=0, bytes_accessed=2 << 20, transcendentals=0),
    )(x, piece)


def inner_call(x, cover, gs, gc, weights):
    frames, row_count, cols, features = x.shape
    rows = frames * HALF * BY
    quads = row_count // HALF - 2
    state = jax.ShapeDtypeStruct((quads, cols // BY, rows, features), BF16)
    return call(
        inner_kernel,
        [HBM, HBM, FULL, FULL, *[HBM] * len(weights)],
        [
            state,
            state,
        ],
        [
            pltpu.VMEM((frames, row_count - BX, cols, features), BF16),
            pltpu.VMEM((cols, COVER_CELLS), jnp.int32),
            *[pltpu.VMEM(w.shape, w.dtype) for w in weights],
        ],
        [pltpu.SemaphoreType.DMA((6,))],
        FULL,
        8000,
        10,
        56,
    )(x, cover, gs, gc, *weights)


def edge_call(row, across, x, cover, gs, gc, weights):
    frames, _, cols, features = x.shape
    rows = frames * HALF * BY
    state = jax.ShapeDtypeStruct((2, cols // BY, rows, features), BF16)
    return call(
        edge_kernel,
        [FULL, FULL, HBM, HBM, FULL, FULL, *[HBM] * 4],
        [state, state],
        [
            pltpu.VMEM((2, frames, HALF, cols, features), BF16),
            pltpu.VMEM((cols, COVER_CELLS), jnp.int32),
            *[pltpu.VMEM(w.shape, w.dtype) for w in weights],
        ],
        [pltpu.SemaphoreType.DMA((7,))],
        FULL,
        6000,
        4,
        48,
    )(row, across, x, cover, gs, gc, *weights)


def cross_call(listed, windows, ckv, cwo, gf, fin, fout, firsts, cqs, frames=4):
    columns, rows, features = firsts[0].shape[1:]
    quads = sum(a.shape[0] for a in firsts)
    out = jax.ShapeDtypeStruct((frames, quads * HALF, columns * BY, features), BF16)
    count = 2 * len(firsts)
    return call(
        functools.partial(cross_kernel, len(firsts)),
        [SCALARS, *[FULL] * 7, HBM, HBM, *[FULL] * count],
        out,
        [
            pltpu.VMEM((sum(w.shape[0] for w in windows), *windows[0].shape[1:]), BF16),
            pltpu.VMEM(out.shape, BF16),
            pltpu.VMEM(fin.shape, BF16),
            pltpu.VMEM(fout.shape, BF16),
        ],
        [pltpu.SemaphoreType.DMA((2,)), pltpu.SemaphoreType.DMA((3,))],
        ANY,
        15000,
        12,
        40,
    )(listed, *windows, ckv, cwo, gf, fin, fout, *firsts, *cqs)


def shards(
    inputs,
    coverage,
    encoded,
    cross_list,
    gain_self,
    gain_cross,
    gain_ffn,
    self_wq,
    self_wkv,
    self_wo,
    cross_wq,
    cross_wkv,
    cross_wo,
    ffn_in,
    ffn_out,
):
    frames, row_count, col_count, features = inputs.shape
    strips = lax.axis_size("gx")
    even = lax.axis_index("gx") % 2 == 0

    def across(s):
        far = s + 1 if s % 2 else s - 1
        return far if 0 <= far < strips else s

    def send(array, target):
        return lax.ppermute(array, ("gx", "gy"), pairs(strips, target))

    def to_row(s, h, c):
        return (s ^ 1, h, c)

    def to_across(s, h, c):
        return (across(s), h, c)

    def to_side(s, h, c):
        return (s, 1 - h, c)

    def to_core(s, h, c):
        return (s, h, 1 - c)

    columns, tokens = encoded.shape[1:3]
    piece = encoded.reshape(columns, HALF, tokens // HALF, features)
    cover = coverage.T
    gs = gain_self.reshape(1, features)
    gc = gain_cross.reshape(1, features)
    weights = (self_wq, self_wkv, self_wo, cross_wq)
    barrier = lax.optimization_barrier

    to_near, to_far = pack_call(inputs, piece)
    got_side = send(piece, to_side)
    got_row = send(to_near, to_row)
    got_across = send(to_far, to_across)
    first_a, cq_a = inner_call(
        inputs,
        cover,
        gs,
        gc,
        weights,
    )
    first_a, cq_a, got_row, got_across, got_side = barrier(
        (first_a, cq_a, got_row, got_across, got_side)
    )
    passed = jnp.concatenate([got_row[frames:], got_across[frames:]], axis=0)
    mine_late = send(passed, to_side)
    mine = jnp.concatenate([piece, got_side, passed], axis=0)
    other = send(mine, to_core)
    first_b, cq_b = edge_call(got_row, got_across, inputs, cover, gs, gc, weights)
    first_b, cq_b, mine_late = barrier((first_b, cq_b, mine_late))
    other_late = send(mine_late, to_core)
    windows = [w.reshape(-1, tokens, features) for w in (mine, mine_late, other, other_late)]
    return cross_call(
        cross_list,
        windows,
        cross_wkv,
        cross_wo,
        gain_ffn.reshape(1, features),
        ffn_in,
        ffn_out,
        [first_a, first_b],
        [cq_a, cq_b],
    )


def solution(mesh):
    return jax.shard_map(
        shards,
        mesh=mesh,
        in_specs=(
            P(None, "gx", "gy", None),
            P(None, "gy"),
            P("gx", "gy", None, None),
            P("gx", "gy", None),
            P(),
            P(),
            P(),
            P(),
            P(),
            P(),
            P(),
            P(),
            P(),
            P(),
            P(),
        ),
        out_specs=P(None, "gx", "gy", None),
        check_vma=False,
    )
```

```python
import functools
import math

import jax
import jax.numpy as jnp
from jax import lax
from jax.experimental import pallas as pl
from jax.experimental.pallas import tpu as pltpu
from jax.sharding import PartitionSpec as P

HEADS = 8
BX = 8
BY = 8
HALF = BX // 2
LOG2E = math.log2(math.e)

epsilon = 1e-05
mask_depth = 30.0

F32 = jnp.float32
BF16 = jnp.bfloat16


def dot(a, b):
    return jnp.dot(a, b, preferred_element_type=F32)


def dot_nt(a, b):
    return lax.dot_general(a, b, (((1,), (1,)), ((), ())), preferred_element_type=F32)


def layer_norm(widened, gain_vec):
    centre = widened - jnp.mean(widened, axis=-1, keepdims=True)
    spread = jnp.mean(centre * centre, axis=-1, keepdims=True)
    return centre * lax.rsqrt(spread + epsilon) * gain_vec


def gelu(v):
    inner = v * (v * v * (math.sqrt(2 / math.pi) * 0.044715) + math.sqrt(2 / math.pi))
    half = 0.5 * v
    return half * jnp.tanh(inner) + half


def granules(block):
    wide = block.astype(F32)
    frames, rows, cols, features = wide.shape
    return [
        wide[:, :, j * BY : (j + 1) * BY].reshape(frames * rows * BY, features)
        for j in range(cols // BY)
    ]


def attend(q, k, v, bias):
    count, features = q.shape
    keys = k.shape[0]
    lane = lax.broadcasted_iota(jnp.int32, (count, 128), 1)
    low = lane < 64
    ones = jnp.ones((keys, 128), BF16)
    zero = jnp.zeros((count, 128), BF16)
    outs = []
    for p in range(features // 128):
        cols = slice(p * 128, p * 128 + 128)
        qp = q[:, cols]
        both = jnp.concatenate([jnp.where(low, qp, zero), jnp.where(low, zero, qp)], axis=0)
        scores = dot_nt(both, k[:, cols])
        if bias is not None:
            scores = scores + bias
        top = jnp.max(scores, axis=-1, keepdims=True)
        weights = jnp.exp2(scores - top).astype(BF16)
        mixed = dot(weights, jnp.concatenate([v[:, cols], ones], axis=1))
        num = jnp.where(low, mixed[:count, :128], mixed[count:, :128])
        den = jnp.where(low, mixed[:count, 128:], mixed[count:, 128:])
        outs.append((num / den).astype(BF16))
    return jnp.concatenate(outs, axis=1)


def position():
    place = lax.axis_index("gy")
    return lax.axis_index("gx"), place // 2, place % 2


def first_cell(strip, row_count, total, window):
    block = jnp.maximum(strip * row_count - HALF, 0) // 128
    return pl.multiple_of(jnp.minimum(block, (total - window) // 128) * 128, 128)


def bias_rows(cover_ref, first_row, quads):
    cols, cells = cover_ref.shape
    cover = cover_ref[...].astype(BF16)
    key = lax.broadcasted_iota(jnp.int32, (128, cells), 0)
    cell = lax.broadcasted_iota(jnp.int32, (128, cells), 1)
    same_row = (cell % HALF) == (key // BY) % HALF
    line = lax.broadcasted_iota(jnp.int32, (8, cells), 0)
    wanted = jnp.full((8, cells), -9, jnp.int32)
    for n, quad in enumerate(quads):
        wanted = jnp.where(line == n, quad, wanted)
    grid_row = lax.broadcasted_iota(jnp.int32, (8, cells), 1) + first_row
    member = jnp.where(grid_row // HALF == wanted, 1.0, 0.0).astype(BF16)
    spot = lax.broadcasted_iota(jnp.int32, (128, cols), 0)
    col = lax.broadcasted_iota(jnp.int32, (128, cols), 1)
    out = []
    for j in range(cols // BY):
        pick = jnp.where(col == j * BY + spot % BY, 1.0, 0.0).astype(BF16)
        spread = jnp.where(same_row, dot(pick, cover), 0.0).astype(BF16)
        out.append((dot_nt(member, spread) - 1.0) * (mask_depth * LOG2E))
    return out


def copies(sems, moves):
    made = [pltpu.make_async_copy(src, dst, sems.at[n]) for n, (src, dst) in enumerate(moves)]
    for copy in made:
        copy.start()
    return made


def pack_kernel(x_hbm, piece_hbm, row_ref, across_ref, sems):
    even = position()[0] % 2 == 0
    frames, row_count = x_hbm.shape[:2]
    last = row_count - HALF
    moves = copies(
        sems,
        [
            (x_hbm.at[:, pl.ds(jnp.where(even, last, 0), HALF)], row_ref.at[:frames]),
            (piece_hbm, row_ref.at[frames:]),
            (x_hbm.at[:, pl.ds(jnp.where(even, 0, last), HALF)], across_ref.at[:frames]),
            (piece_hbm, across_ref.at[frames:]),
        ],
    )
    for move in moves:
        move.wait()


def shifted_attention(strip, cover_buf, start, quads, cuboids, parts, halo, gs, gc, wq, wkv, wo, cwq, moves=()):
    features = wq.shape[0]
    rows = parts[0].shape[0]
    base = jnp.concatenate(parts, axis=0)
    normed = layer_norm(base, gs).astype(BF16)
    every = normed if halo is None else jnp.concatenate([normed, halo], axis=0)
    for move in moves[:3]:
        move.wait()
    bias = bias_rows(cover_buf, start, quads)
    kv = dot(every, wkv[...]).astype(BF16)
    q = (dot(normed, wq[...]) * (LOG2E / 8.0)).astype(BF16)

    def pick(a, which):
        return jnp.concatenate([a[n * rows : (n + 1) * rows] for n in which], axis=0)

    mixed = [None] * len(parts)
    for keys, queries, lines, j in cuboids:
        keep = jnp.concatenate([bias[j][n : n + 1] for n in lines], axis=1)
        kvj = pick(kv, keys)
        out = attend(pick(q, queries), kvj[:, :features], kvj[:, features:], keep)
        for n, g in enumerate(queries):
            mixed[g] = out[n * rows : (n + 1) * rows]
    for move in moves[3:]:
        move.wait()
    first = (base + dot(jnp.concatenate(mixed, axis=0), wo[...])).astype(BF16)
    normed = layer_norm(first.astype(F32), gc).astype(BF16)
    return first, (dot(normed, cwq[...]) * (LOG2E / 8.0)).astype(BF16)


def inner_kernel(
    x_hbm, cover_hbm, gs_ref, gc_ref, wq_hbm, wkv_hbm, wo_hbm, cwq_hbm,
    first_ref, cq_ref,
    x_buf, cover_ref, wq, wkv, wo, cwq, sems,
):
    strip = position()[0]
    row_count = x_hbm.shape[1]
    last = row_count - HALF
    start = first_cell(strip, row_count, cover_hbm.shape[1], cover_ref.shape[1])
    inner = x_buf.shape[1]
    moves = copies(
        sems,
        [
            (x_hbm.at[:, HALF:last], x_buf),
            (wkv_hbm, wkv),
            (cover_hbm.at[:, pl.ds(start, cover_ref.shape[1])], cover_ref),
            (wq_hbm, wq),
            (wo_hbm, wo),
            (cwq_hbm, cwq),
        ],
    )
    moves[0].wait()
    parts, quads, cuboids = [], [], []
    for t in range(inner // HALF):
        parts += granules(x_buf[:, t * HALF : (t + 1) * HALF])
        quads.append(strip * (row_count // HALF) + 1 + t)
    for c in range(inner // BX):
        for j in range(2):
            pair = (4 * c + j, 4 * c + 2 + j)
            cuboids.append((pair, pair, (2 * c, 2 * c + 1), j))
    first, cq = shifted_attention(
        strip,
        cover_ref,
        start,
        quads,
        cuboids,
        parts,
        None,
        gs_ref[...],
        gc_ref[...],
        wq,
        wkv,
        wo,
        cwq,
        moves[1:6],
    )
    first_ref[...] = first.reshape(first_ref.shape)
    cq_ref[...] = cq.reshape(cq_ref.shape)
    for move in moves[6:]:
        move.wait()


def edge_kernel(
    row_ref, across_ref, x_hbm, cover_hbm, gs_ref, gc_ref, wq_hbm, wkv_hbm, wo_hbm, cwq_hbm,
    first_ref, cq_ref, sides_ref, cover_ref, wq, wkv, wo, cwq, sems,
):
    strip = position()[0]
    row_count = x_hbm.shape[1]
    per_strip = row_count // HALF
    strips = lax.axis_size("gx")
    even = strip % 2 == 0
    frames = sides_ref.shape[1]
    start = first_cell(strip, row_count, cover_hbm.shape[1], cover_ref.shape[1])
    last = row_count - HALF
    moves = copies(
        sems,
        [
            (x_hbm.at[:, pl.ds(jnp.where(even, last, 0), HALF)], sides_ref.at[0]),
            (x_hbm.at[:, pl.ds(jnp.where(even, 0, last), HALF)], sides_ref.at[1]),
            (cover_hbm.at[:, pl.ds(start, cover_ref.shape[1])], cover_ref),
            (wkv_hbm, wkv),
            (wq_hbm, wq),
            (wo_hbm, wo),
            (cwq_hbm, cwq),
        ],
    )
    for move in moves[:2]:
        move.wait()
    gs = gs_ref[...]
    parts, quads, cuboids, halos = [], [], [], []
    for n, halo_ref in enumerate((row_ref, across_ref)):
        above = even if n == 0 else jnp.logical_not(even)
        parts += granules(sides_ref[n])
        own = strip * per_strip + jnp.where(above, per_strip - 1, 0)
        quads += [own, own + jnp.where(above, 1, -1)]
        halo = layer_norm(jnp.concatenate(granules(halo_ref[:frames]), axis=0), gs)
        outside = jnp.where(above, strip == strips - 1, strip == 0)
        halos.append((halo * jnp.where(outside, 0.0, 1.0)).astype(BF16))
        for j in range(2):
            g = 2 * n + j
            cuboids.append(((g, 4 + g), (g,), (2 * n, 2 * n + 1), j))
    first, cq = shifted_attention(
        strip,
        cover_ref,
        start,
        quads,
        cuboids,
        parts,
        jnp.concatenate(halos, axis=0),
        gs,
        gc_ref[...],
        wq,
        wkv,
        wo,
        cwq,
        moves[2:],
    )
    first_ref[...] = first.reshape(first_ref.shape)
    cq_ref[...] = cq.reshape(cq_ref.shape)


def cross_kernel(states, list_ref, w0_ref, w1_ref, w2_ref, w3_ref, w4_ref, w5_ref, ckv_ref, cwo_ref, gf_ref, fin_hbm, fout_hbm, *refs):
    first_refs, cq_refs, refs = refs[:states], refs[states : 2 * states], refs[2 * states :]
    out_hbm, window, out_buf, fin_ref, fout_ref, sems, out_sems = refs
    moves = copies(sems, [(fin_hbm, fin_ref), (fout_hbm, fout_ref)])
    strip, side, core = position()
    features = cwo_ref.shape[0]
    tiles = out_hbm.shape[1] // BX

    def granule(refs, quad, j):
        inner, edges = refs
        at_top = strip % 2 == 0
        if quad == 0:
            return edges[jnp.where(at_top, 1, 0), j]
        if quad == 2 * tiles - 1:
            return edges[jnp.where(at_top, 0, 1), j]
        return inner[quad - 1, j]

    at = 0
    for part in (w0_ref, w1_ref, w2_ref, w3_ref, w4_ref, w5_ref):
        window[at : at + part.shape[0]] = part[...]
        at += part.shape[0]
    toward_row = jnp.where(strip % 2 == 0, 1, -1)

    def entry(n):
        e = list_ref[n // 8, n // 4 % 2, n % 4]
        delta = e // 8 - strip
        column = e % 8
        e_side, e_core, sub = column // 4, (column // 2) % 2, column % 2
        same = e_side == side
        near = jnp.where(delta == toward_row, 0, 1)
        slot = jnp.where(same, 2, 4) + near
        slot = jnp.where(delta == 0, jnp.where(same, 0, 1), slot)
        half = window.shape[0] // 2
        return window[jnp.where(e_core == core, 0, half) + slot * 2 + sub]

    kvs = []
    for n in range(2 * tiles):
        chosen = jnp.concatenate([entry(n * 4 + l) for l in range(4)], axis=0)
        kvs.append(dot(chosen, ckv_ref[...]).astype(BF16))
    mixed = []
    for k in range(tiles):
        for j in range(2):
            kv = kvs[2 * k + j]
            q = jnp.concatenate([granule(cq_refs, 2 * k + t, j) for t in range(2)], axis=0)
            mixed.append(attend(q, kv[:, :features], kv[:, features:], None))
    for move in moves:
        move.wait()
    outs = []
    hidden_units = fin_ref.shape[1]
    step = 2048
    frames = out_buf.shape[0]
    for k in range(tiles):
        first = jnp.concatenate(
            [granule(first_refs, 2 * k + t, j) for j in range(2) for t in range(2)], axis=0
        )
        both = jnp.concatenate(mixed[2 * k : 2 * k + 2], axis=0)
        second = (first.astype(F32) + dot(both, cwo_ref[...])).astype(BF16).astype(F32)
        normed = layer_norm(second, gf_ref[...]).astype(BF16)
        total = second
        for c in range(0, hidden_units, step):
            hidden = gelu(dot(normed, fin_ref[:, c : c + step])).astype(BF16)
            total = total + dot(hidden, fout_ref[c : c + step, :])
        shaped = total.reshape(2, 2, frames, HALF, BY, features)
        cols = jnp.concatenate([shaped[0], shaped[1]], axis=3).astype(BF16)
        out_buf[:, k * BX : k * BX + HALF] = cols[0]
        out_buf[:, k * BX + HALF : (k + 1) * BX] = cols[1]
        here = slice(k * BX, (k + 1) * BX)
        outs.append(pltpu.make_async_copy(out_buf.at[:, here], out_hbm.at[:, here], out_sems.at[k]))
        outs[-1].start()
    for copy in outs:
        copy.wait()


def pairs(strips, target):
    out = []
    for s in range(strips):
        for h in range(2):
            for c in range(2):
                s2, h2, c2 = target(s, h, c)
                out.append((s * 4 + h * 2 + c, s2 * 4 + h2 * 2 + c2))
    return out


ANY = pl.BlockSpec(memory_space=pl.ANY)
HBM = pl.BlockSpec(memory_space=pltpu.HBM)
SCALARS = pl.BlockSpec(memory_space=pltpu.SMEM)
FULL = pl.BlockSpec(memory_space=pltpu.VMEM)
COVER_CELLS = 256


def call(kernel, kinds, out_shape, scratch, sems, out_kind, mflops, mbytes, limit):
    return pl.pallas_call(
        kernel,
        in_specs=kinds,
        out_specs=jax.tree.map(lambda _: out_kind, out_shape),
        out_shape=out_shape,
        scratch_shapes=[*scratch, *sems],
        compiler_params=pltpu.CompilerParams(vmem_limit_bytes=limit << 20),
        cost_estimate=pl.CostEstimate(
            flops=mflops * 10**6, bytes_accessed=mbytes << 20, transcendentals=0
        ),
    )


def pack_call(x, piece):
    frames, _, cols, features = x.shape
    out = jax.ShapeDtypeStruct((frames + piece.shape[0], HALF, cols, features), BF16)
    return pl.pallas_call(
        pack_kernel,
        in_specs=[ANY, ANY],
        out_specs=[FULL, FULL],
        out_shape=[out, out],
        scratch_shapes=[pltpu.SemaphoreType.DMA((4,))],
        cost_estimate=pl.CostEstimate(flops=0, bytes_accessed=2 << 20, transcendentals=0),
    )(x, piece)


def inner_call(x, cover, gs, gc, weights):
    frames, row_count, cols, features = x.shape
    rows = frames * HALF * BY
    quads = row_count // HALF - 2
    state = jax.ShapeDtypeStruct((quads, cols // BY, rows, features), BF16)
    return call(
        inner_kernel,
        [HBM, HBM, FULL, FULL, *[HBM] * len(weights)],
        [
            state,
            state,
        ],
        [
            pltpu.VMEM((frames, row_count - BX, cols, features), BF16),
            pltpu.VMEM((cols, COVER_CELLS), jnp.int32),
            *[pltpu.VMEM(w.shape, w.dtype) for w in weights],
        ],
        [pltpu.SemaphoreType.DMA((6,))],
        FULL,
        8000,
        10,
        56,
    )(x, cover, gs, gc, *weights)


def edge_call(row, across, x, cover, gs, gc, weights):
    frames, _, cols, features = x.shape
    rows = frames * HALF * BY
    state = jax.ShapeDtypeStruct((2, cols // BY, rows, features), BF16)
    return call(
        edge_kernel,
        [FULL, FULL, HBM, HBM, FULL, FULL, *[HBM] * 4],
        [state, state],
        [
            pltpu.VMEM((2, frames, HALF, cols, features), BF16),
            pltpu.VMEM((cols, COVER_CELLS), jnp.int32),
            *[pltpu.VMEM(w.shape, w.dtype) for w in weights],
        ],
        [pltpu.SemaphoreType.DMA((7,))],
        FULL,
        6000,
        4,
        48,
    )(row, across, x, cover, gs, gc, *weights)


def cross_call(listed, windows, ckv, cwo, gf, fin, fout, firsts, cqs, frames=4):
    columns, rows, features = firsts[0].shape[1:]
    quads = sum(a.shape[0] for a in firsts)
    out = jax.ShapeDtypeStruct((frames, quads * HALF, columns * BY, features), BF16)
    count = 2 * len(firsts)
    return call(
        functools.partial(cross_kernel, len(firsts)),
        [SCALARS, *[FULL] * 9, HBM, HBM, *[FULL] * count],
        out,
        [
            pltpu.VMEM((sum(w.shape[0] for w in windows), *windows[0].shape[1:]), BF16),
            pltpu.VMEM(out.shape, BF16),
            pltpu.VMEM(fin.shape, BF16),
            pltpu.VMEM(fout.shape, BF16),
        ],
        [pltpu.SemaphoreType.DMA((2,)), pltpu.SemaphoreType.DMA((3,))],
        ANY,
        15000,
        12,
        40,
    )(listed, *windows, ckv, cwo, gf, fin, fout, *firsts, *cqs)


def shards(
    inputs,
    coverage,
    encoded,
    cross_list,
    gain_self,
    gain_cross,
    gain_ffn,
    self_wq,
    self_wkv,
    self_wo,
    cross_wq,
    cross_wkv,
    cross_wo,
    ffn_in,
    ffn_out,
):
    frames, row_count, col_count, features = inputs.shape
    strips = lax.axis_size("gx")
    even = lax.axis_index("gx") % 2 == 0

    def across(s):
        far = s + 1 if s % 2 else s - 1
        return far if 0 <= far < strips else s

    def send(array, target):
        return lax.ppermute(array, ("gx", "gy"), pairs(strips, target))

    def to_row(s, h, c):
        return (s ^ 1, h, c)

    def to_across(s, h, c):
        return (across(s), h, c)

    def to_side(s, h, c):
        return (s, 1 - h, c)

    def to_core(s, h, c):
        return (s, h, 1 - c)

    columns, tokens = encoded.shape[1:3]
    piece = encoded.reshape(columns, HALF, tokens // HALF, features)
    cover = coverage.T
    gs = gain_self.reshape(1, features)
    gc = gain_cross.reshape(1, features)
    weights = (self_wq, self_wkv, self_wo, cross_wq)
    barrier = lax.optimization_barrier

    to_near, to_far = pack_call(inputs, piece)
    got_side = send(piece, to_side)
    got_row = send(to_near, to_row)
    got_across = send(to_far, to_across)
    first_a, cq_a = inner_call(
        inputs,
        cover,
        gs,
        gc,
        weights,
    )
    first_a, cq_a, got_row, got_side = barrier((first_a, cq_a, got_row, got_side))
    row_piece = got_row[frames:]
    late_row = send(row_piece, to_side)
    mine = jnp.concatenate([piece, got_side, row_piece], axis=0)
    other = send(mine, to_core)
    got_across, first_a, cq_a = barrier((got_across, first_a, cq_a))
    across_piece = got_across[frames:]
    late_across = send(across_piece, to_side)
    other_across = send(across_piece, to_core)
    first_b, cq_b = edge_call(got_row, got_across, inputs, cover, gs, gc, weights)
    first_b, cq_b, late_row, late_across = barrier((first_b, cq_b, late_row, late_across))
    late = jnp.concatenate([late_row, late_across], axis=0)
    other_late = send(late, to_core)
    windows = [mine, across_piece, late, other, other_across, other_late]
    windows = [w.reshape(-1, tokens, features) for w in windows]
    return cross_call(
        cross_list,
        windows,
        cross_wkv,
        cross_wo,
        gain_ffn.reshape(1, features),
        ffn_in,
        ffn_out,
        [first_a, first_b],
        [cq_a, cq_b],
    )


def solution(mesh):
    return jax.shard_map(
        shards,
        mesh=mesh,
        in_specs=(
            P(None, "gx", "gy", None),
            P(None, "gy"),
            P("gx", "gy", None, None),
            P("gx", "gy", None),
            P(),
            P(),
            P(),
            P(),
            P(),
            P(),
            P(),
            P(),
            P(),
            P(),
            P(),
        ),
        out_specs=P(None, "gx", "gy", None),
        check_vma=False,
    )
```
